32 devices in a mesh: wide: 8 (over z, y), narrow: 4 (over x, core).
Axes of the slice: x: 2, y: 2, z: 4, core: 2. Of those that a mesh axis runs over, the one named last changes fastest.
Arguments:
- resid: bfloat16 [2, 32, 1024, 767], P(None, ('wide', 'narrow')), may hold values from -6 to 6
- lengths: int32 [2, 32, 8], P(None, ('wide', 'narrow')), may hold values from 1 to 512, 1024 in all within a row
- pad_len: int32 [2, 32], P(None, ('wide', 'narrow')), may hold values from 0 to 128
- gain_attn: bfloat16 [768], P(('wide', 'narrow')), may hold values from 0.099609375 to 1.8984375
- w_qkv: bfloat16 [768, 2304], P(('wide', 'narrow')), may hold values from -0.21875 to 0.21875
- b_query: bfloat16 [768], P(('wide', 'narrow')), may hold values from -3 to 3
- b_value: bfloat16 [768], P(('wide', 'narrow')), may hold values from -3 to 3
- w_out: bfloat16 [768, 768], P(('wide', 'narrow')), may hold values from -0.875 to 0.875
- b_out: bfloat16 [768], P(('wide', 'narrow')), may hold values from -2 to 2
- gain_mlp: bfloat16 [768], P(('wide', 'narrow')), may hold values from 0.099609375 to 1.8984375
- w_up: bfloat16 [768, 3072], P(('wide', 'narrow')), may hold values from -0.21875 to 0.21875
- b_up: bfloat16 [3072], P(('wide', 'narrow')), may hold values from -3 to 3
- w_down: bfloat16 [3072, 768], P(('wide', 'narrow')), may hold values from -0.109375 to 0.109375
- b_down: bfloat16 [768], P(('wide', 'narrow')), may hold values from -2 to 2
- cotangent: bfloat16 [2, 32, 1024, 767], P(None, ('wide', 'narrow')), may hold values from -6 to 6
Outputs:
- resid_out: bfloat16 [2, 32, 1024, 767], P(None, ('wide', 'narrow'))
- grad_resid: bfloat16 [2, 32, 1024, 767], P(None, ('wide', 'narrow'))
- grad_gain_attn: float32 [768], P(('wide', 'narrow'))
- grad_w_qkv: float32 [768, 2304], P(('wide', 'narrow'))
- grad_b_query: float32 [768], P(('wide', 'narrow'))
- grad_b_value: float32 [768], P(('wide', 'narrow'))
- grad_w_out: float32 [768, 768], P(('wide', 'narrow'))
- grad_b_out: float32 [768], P(('wide', 'narrow'))
- grad_gain_mlp: float32 [768], P(('wide', 'narrow'))
- grad_w_up: float32 [768, 3072], P(('wide', 'narrow'))
- grad_b_up: float32 [3072], P(('wide', 'narrow'))
- grad_w_down: float32 [3072, 768], P(('wide', 'narrow'))
- grad_b_down: float32 [768], P(('wide', 'narrow'))
The draws below stay inside these ranges and needn't reach their ends.
Inputs may be any that keep to these rules, and one draw needn't show every extreme that they name: In each row the 8 document lengths sum to 1024.
All inputs are finite; a program needn't handle non-finite values.
Results may differ from the reference program's by a relative error of at most 0.011.
Values may be sent and summed in bfloat16 or wider, within the bound.
A program may use at most 384 MiB of HBM per device.

```python
import math
import jax
import jax.numpy as jnp
import numpy as np
from jax import lax

D = 768
HEADS = 12
FF = 3072
HD = 64
DC = 767
SEQ = 1024
MICRO = 2
DOCS = 8
MOST = 512
PADMAX = 128
ROWS = 32


def plant(array, key, low, high):
    spot = [jax.random.randint(jax.random.fold_in(key, axis), (), 0, length) for axis, length in enumerate(array.shape)]
    main_axis = array.shape.index(max(array.shape))
    beside = spot[:main_axis] + [(spot[main_axis] + 1) % array.shape[main_axis]] + spot[main_axis + 1:]
    return array.at[tuple(spot)].set(low).at[tuple(beside)].set(high)


def block_scale(rng, shape, split, low, top_value):
    level = 1.0
    for dim, parts in split:
        draws = jax.random.uniform(jax.random.fold_in(jax.random.fold_in(rng, 6), dim), (parts,), jnp.float32, low / len(split), top_value / len(split))
        level = level * jnp.repeat(jnp.exp(draws), shape[dim] // parts).reshape((-1,) + (1,) * (len(shape) - 1 - dim))
    return level


def profile(count, total, most, slope):
    portions = [(1 << 20) // math.isqrt(grade ** slope) + 1 for grade in range(2, count + 1)]
    spare, holding = total - most - (count - 1), [1] * (count - 1)
    while spare > 0:
        movable = [i for i in range(count - 1) if holding[i] < most]
        pool, remaining = sum([portions[i] for i in movable]), spare
        for i in movable:
            addition = min(most - holding[i], max(1, remaining * portions[i] // pool), spare)
            holding[i] = holding[i] + addition
            spare = spare - addition
    return np.array([most] + holding)


def ragged_sizes(key, amount, total, reach, skew):
    if amount == 2:
        one = jax.random.randint(key, (), max(1, total - reach), min(reach, total - 1) + 1)
        return jnp.stack([one, total - one])
    sizes = jnp.asarray(profile(amount, total, reach, skew), jnp.int32)
    couples = (amount - 1) // 2
    donor, sink = sizes[1:1 + 2 * couples:2], sizes[2:2 + 2 * couples:2]
    room = jnp.minimum(donor - 1, reach - sink)
    passed = jax.random.randint(jax.random.fold_in(key, 1), (couples,), 0, 1 << 20) % (room + 1)
    sizes = sizes.at[1:1 + 2 * couples:2].set(donor - passed).at[2:2 + 2 * couples:2].set(sink + passed)
    return sizes[jax.random.permutation(jax.random.fold_in(key, 2), amount)]


def scatter_about(rng, dims, width, bound, pieces=(), kind=jnp.bfloat16):
    values = jax.random.normal(rng, dims, jnp.float32) * width
    if len(pieces) > 0:
        values = block_scale(rng, dims, pieces, -0.22, 0.18) * values
    return jnp.clip(values, min=-bound, max=bound).astype(kind)


def setup_inputs(seed: int = 0) -> dict:
    keys = jax.random.split(jax.random.key(seed), 16)
    return {
        "resid": scatter_about(keys[0], (MICRO, ROWS, SEQ, DC), 1.0, 6.0, ((1, 32),)),
        "lengths": jax.vmap(lambda own: ragged_sizes(own, DOCS, SEQ, MOST, 2))(jax.random.split(keys[1], MICRO * ROWS)).reshape((MICRO, ROWS, DOCS)).astype(jnp.int32),
        "pad_len": plant(jax.random.randint(keys[2], (MICRO, ROWS), 0, PADMAX + 1), jax.random.fold_in(keys[2], 1), 0, PADMAX).astype(jnp.int32),
        "gain_attn": jnp.clip(1.0 + 0.18 * jax.random.normal(keys[3], (D,), jnp.float32), 0.099609375, 1.8984375).astype(jnp.bfloat16),
        "w_qkv": scatter_about(keys[4], (D, 3 * D), D ** -0.5, 0.21875, ((0, 32),)),
        "b_query": scatter_about(keys[5], (D,), 0.5, 3.0, ((0, 32),)),
        "b_value": scatter_about(keys[6], (D,), 0.5, 3.0, ((0, 32),)),
        "w_out": scatter_about(keys[7], (D, D), (D // 16) ** -0.5, 0.875, ((0, 32),)),
        "b_out": scatter_about(keys[8], (D,), 0.3, 2.0, ((0, 32),)),
        "gain_mlp": jnp.clip(1.0 + 0.18 * jax.random.normal(keys[9], (D,), jnp.float32), 0.099609375, 1.8984375).astype(jnp.bfloat16),
        "w_up": scatter_about(keys[10], (D, FF), D ** -0.5, 0.21875, ((0, 32),)),
        "b_up": scatter_about(keys[11], (FF,), 0.5, 3.0, ((0, 32),)),
        "w_down": scatter_about(keys[12], (FF, D), FF ** -0.5, 0.109375, ((0, 32),)),
        "b_down": scatter_about(keys[13], (D,), 0.3, 2.0, ((0, 32),)),
        "cotangent": scatter_about(keys[14], (MICRO, ROWS, SEQ, DC), 1.0, 6.0, ((1, 32),)),
    }


@jax.custom_vjp
def low(v):
    return lax.optimization_barrier(v.astype(jnp.bfloat16)).astype(jnp.float32)

@jax.custom_vjp
def low_back(v):
    return v

def low_keep(v):
    return (low(v), None)

def low_pass(kept, grad):
    return (grad,)

def back_keep(v):
    return (v, None)

def back_low(kept, grad):
    return (low(grad),)
low.defvjp(low_keep, low_pass)
low_back.defvjp(back_keep, back_low)

def matmul_hi(left, right):
    return jnp.dot(left, right, precision=lax.Precision.HIGHEST, preferred_element_type=jnp.float32)

def decompress(compact):
    return jnp.concatenate([compact, -lax.optimization_barrier(jnp.sum(compact, axis=-1, keepdims=True))], axis=-1)

def crms_norm(whole_vec, gain):
    factor = lax.rsqrt(lax.optimization_barrier(jnp.mean(whole_vec * whole_vec, axis=-1, keepdims=True)) + 1e-05)
    return whole_vec * factor * gain

def centered(branch):
    return branch - lax.optimization_barrier(jnp.mean(branch, axis=-1, keepdims=True))

def segment_ids(doc_lengths, pad_count):
    doc_ends = jnp.cumsum(doc_lengths)
    positions = jnp.arange(SEQ, dtype=jnp.int32)
    counted = lax.optimization_barrier(jnp.sum((doc_ends[None, :] <= positions[:, None]).astype(jnp.int32), axis=1))
    return jnp.where(positions >= SEQ - pad_count, DOCS + positions, counted).astype(jnp.int32)

def attend(query_vecs, key_vecs, value_vecs, segments):
    block_rows = min(512, SEQ)
    block_count = SEQ // block_rows
    query_blocks = query_vecs.reshape(block_count, block_rows, HEADS, HD)
    offsets = jnp.arange(block_count, dtype=jnp.int32) * block_rows
    key_pos = jnp.arange(SEQ, dtype=jnp.int32)

    def block_fn(item):
        query_part, offset = item
        query_pos = offset + jnp.arange(block_rows, dtype=jnp.int32)
        query_seg = lax.dynamic_slice_in_dim(segments, offset, block_rows)
        allowed = (key_pos[None, :] <= query_pos[:, None]) & (segments[None, :] == query_seg[:, None])
        scores = jnp.einsum('qhd,khd->hqk', query_part, key_vecs, precision=lax.Precision.HIGHEST) * HD ** (-0.5)
        scores = low_back(scores)
        scores = jnp.where(allowed[None], scores, -1e+30)
        attn_probs = low(jax.nn.softmax(scores, axis=-1))
        return jnp.einsum('hqk,khd->qhd', attn_probs, value_vecs, precision=lax.Precision.HIGHEST)
    return lax.map(jax.checkpoint(block_fn), (query_blocks, offsets)).reshape(SEQ, D)

def layer_row(compact, segments, params):
    gain_attn, w_qkv, b_query, b_value, w_out, b_out, gain_mlp, w_up, b_up, w_down, b_down = params
    whole_first = decompress(compact)
    normed_first = low(crms_norm(whole_first, gain_attn))
    qkv_mixed = low_back(matmul_hi(normed_first, w_qkv))
    query_vecs = low(qkv_mixed[:, :D] + b_query).reshape(SEQ, HEADS, HD)
    key_vecs = low(qkv_mixed[:, D:2 * D]).reshape(SEQ, HEADS, HD)
    value_vecs = low(qkv_mixed[:, 2 * D:] + b_value).reshape(SEQ, HEADS, HD)
    attended = low(low_back(attend(query_vecs, key_vecs, value_vecs, segments)))
    branch_first = centered(low_back(matmul_hi(attended, w_out)) + b_out)
    middle = compact + branch_first[:, :DC]
    whole_second = decompress(middle)
    normed_second = low(crms_norm(whole_second, gain_mlp))
    hidden = low_back(matmul_hi(normed_second, w_up)) + b_up
    active = low(jax.nn.gelu(hidden, approximate=True))
    branch_second = centered(low_back(matmul_hi(active, w_down)) + b_down)
    return middle + branch_second[:, :DC]

def reference(resid, lengths, pad_len, gain_attn, w_qkv, b_query, b_value, w_out, b_out, gain_mlp, w_up, b_up, w_down, b_down, cotangent):
    params = (gain_attn.astype(jnp.float32), w_qkv.astype(jnp.float32), b_query.astype(jnp.float32), b_value.astype(jnp.float32), w_out.astype(jnp.float32), b_out.astype(jnp.float32), gain_mlp.astype(jnp.float32), w_up.astype(jnp.float32), b_up.astype(jnp.float32), w_down.astype(jnp.float32), b_down.astype(jnp.float32))
    row_inputs = resid.astype(jnp.float32).reshape(-1, SEQ, DC)
    segments = jax.vmap(segment_ids)(lengths.reshape(-1, DOCS), pad_len.reshape(-1))

    def forward(row_values, param_values):

        def row_fn(item):
            return layer_row(item[0], item[1], param_values)
        return lax.map(jax.checkpoint(row_fn), (row_values, segments))
    outputs, pullback = jax.vjp(forward, row_inputs, params)
    grad_rows, grad_params = pullback(cotangent.astype(jnp.float32).reshape(-1, SEQ, DC))
    full_shape = resid.shape
    return (outputs.astype(jnp.bfloat16).reshape(full_shape), grad_rows.astype(jnp.bfloat16).reshape(full_shape), grad_params[0], grad_params[1], grad_params[2], grad_params[3], grad_params[4], grad_params[5], grad_params[6], grad_params[7], grad_params[8], grad_params[9], grad_params[10])
```

```python
import functools
import math
import jax
import jax.numpy as jnp
from jax import lax
from jax.experimental import pallas as pl
from jax.experimental.pallas import tpu as pltpu
from jax.sharding import PartitionSpec as P

F32 = jnp.float32
BF16 = jnp.bfloat16
epsilon = 1e-05
vmem_grant = 60 << 20
NT = (((1,), (1,)), ((), ()))
TN = (((0,), (0,)), ((), ()))
NN = (((1,), (0,)), ((), ()))
gelu_c0 = math.sqrt(2.0 / math.pi)
gelu_c1 = gelu_c0 * 0.044715


def dot(left, right, dims=NN):
    return lax.dot_general(left, right, dims, preferred_element_type=F32)


def lane_index(shape):
    return lax.broadcasted_iota(jnp.int32, shape, 1)


def row_sum(values):
    return jnp.sum(values, axis=1, keepdims=True)


AX = ("wide", "narrow")
HEADS = 12
MOST = 512
masked_score = -1e30


MESH = pl.DeviceIdType.MESH


class Place:
    def __init__(self, nz, ny, nx):
        self.nz, self.ny, self.nx = nz, ny, nx
        wide = lax.axis_index("wide")
        narrow = lax.axis_index("narrow")
        self.z, self.y = wide // ny, wide % ny
        self.x, self.c = narrow // 2, narrow % 2

    def block(self, third, second, deep):
        along_y = jnp.where(self.c == 0, second, third)
        along_x = jnp.where(self.c == 0, third, second)
        return (self.z + deep) % self.nz, (self.y + along_y) % self.ny, (self.x + along_x) % self.nx

    def device(self, third, second, deep, other_core=False):
        z, y, x = self.block(third, second, deep)
        core = 1 - self.c if other_core else self.c
        return (z * self.ny + y, x * 2 + core)

    def greet(self):
        barrier = pltpu.get_barrier_semaphore()
        partners = [self.device(0, 0, k) for k in range(1, self.nz)]
        partners += [self.device(0, k, 0) for k in range(1, self.nx)]
        partners += [self.device(k, 0, 0) for k in range(1, self.nx)]
        partners.append(self.device(0, 0, 0, True))
        for partner in partners:
            pl.semaphore_signal(barrier, inc=1, device_id=partner, device_id_type=MESH)
        pl.semaphore_wait(barrier, len(partners))


class Transfer:
    def __init__(self, place, send, recv):
        self.place, self.send, self.recv = place, send, recv
        self.index = {key: n for n, key in enumerate(self.keys(place.nz, place.nx))}

    def copy(self, key):
        source, target, device = self.ends(key)
        n = self.index[key]
        return pltpu.make_async_remote_copy(
            src_ref=source,
            dst_ref=target,
            send_sem=self.send.at[n],
            recv_sem=self.recv.at[n],
            device_id=device,
            device_id_type=MESH,
        )

    def start(self, *key):
        self.copy(key).start()

    def arrived(self, *key):
        self.copy(key).wait_recv()

    def sent(self):
        for key in self.index:
            self.copy(key).wait_send()


class Gather(Transfer):
    def __init__(self, place, shard, full, send, recv, local):
        super().__init__(place, send, recv)
        self.shard, self.full, self.local = shard, full, local

    @staticmethod
    def keys(nz, n2):
        out = [("z", k) for k in range(1, nz)]
        out += [("s", k, d) for k in range(1, n2) for d in range(nz)]
        out += [("t", k, b, d) for k in range(1, n2) for b in range(n2) for d in range(nz)]
        out += [("c", a, b, d) for a in range(n2) for b in range(n2) for d in range(nz)]
        return out

    def ends(self, key):
        p = self.place
        kind = key[0]
        if kind == "z":
            offset, device = (0, 0, 0), p.device(0, 0, key[1])
        elif kind == "s":
            offset, device = (0, 0, key[2]), p.device(0, key[1], 0)
        elif kind == "t":
            offset, device = (0, key[2], key[3]), p.device(key[1], 0, 0)
        else:
            offset, device = key[1:], p.device(0, 0, 0, True)
        z, y, x = p.block(*offset)
        target = self.full.at[z, y, x, p.c]
        return (self.shard if offset == (0, 0, 0) else target), target, device

    def own(self):
        p = self.place
        return pltpu.make_async_copy(self.shard, self.full.at[p.z, p.y, p.x, p.c], self.local)

    def spread(self, a, b, d):
        if a == 0:
            if b == 0:
                for k in range(1, self.place.nx):
                    self.start("s", k, d)
            for k in range(1, self.place.nx):
                self.start("t", k, b, d)
        self.start("c", a, b, d)

    def begin(self):
        for k in range(1, self.place.nz):
            self.start("z", k)
        self.spread(0, 0, 0)
        self.own().start()

    def steps(self):
        nz, n2 = self.place.nz, self.place.nx

        def step(key, a, b, d):
            def run():
                self.arrived(*key)
                self.spread(a, b, d)

            return run

        out = [step(("z", k), 0, 0, nz - k) for k in range(1, nz)]
        order = [0] + [nz - k for k in range(1, nz)]
        out += [step(("s", k, d), 0, n2 - k, d) for d in order for k in range(1, n2)]
        out += [
            step(("t", k, b, d), n2 - k, b, d) for b in range(n2) for d in order for k in range(1, n2)
        ]
        return out

    def landed(self):
        for key in self.index:
            if key[0] == "c":
                self.arrived(*key)
        self.own().wait()


class Scatter(Transfer):
    def __init__(self, place, terms, out, buffers, send, recv, load):
        super().__init__(place, send, recv)
        self.terms, self.out = terms, out
        self.mine, self.r0, self.r1, self.r2, self.r3 = buffers
        self.load = load

    @staticmethod
    def keys(nz, n2):
        out = [("c", a, b, d) for a in range(n2) for b in range(n2) for d in range(nz)]
        out += [("t", a, b, d) for a in range(1, n2) for b in range(n2) for d in range(nz)]
        out += [("s", b, d) for b in range(1, n2) for d in range(nz)]
        out += [("z", d) for d in range(1, nz)]
        return out

    @staticmethod
    def buffers(nz, n2, block, dtype):
        counts = (nz * n2 * n2, nz * n2 * n2, nz * n2 * (n2 - 1), nz * (n2 - 1), nz - 1)
        return [pltpu.VMEM((n,) + block, dtype) for n in counts]

    def slot(self, a, b, d):
        return (a * self.place.nx + b) * self.place.nz + d

    def order(self):
        near = list(range(1, self.place.nx)) + [0]
        deep = list(range(1, self.place.nz)) + [0]
        return [(a, b, d) for a in near for b in near for d in deep]

    def ends(self, key):
        p = self.place
        kind = key[0]
        if kind == "c":
            a, b, d = key[1:]
            z, y, x = p.block(a, b, d)
            return self.terms.at[z, y, x, 1 - p.c], self.r0.at[self.slot(b, a, d)], p.device(0, 0, 0, True)
        if kind == "t":
            a, b, d = key[1:]
            return self.mine.at[self.slot(a, b, d)], self.r1.at[self.slot(a - 1, b, d)], p.device(a, 0, 0)
        if kind == "s":
            b, d = key[1:]
            return self.mine.at[self.slot(0, b, d)], self.r2.at[self.slot(0, b - 1, d)], p.device(0, b, 0)
        d = key[1]
        return self.mine.at[self.slot(0, 0, d)], self.r3.at[d - 1], p.device(0, 0, d)

    def loading(self, a, b, d):
        p = self.place
        z, y, x = p.block(a, b, d)
        n = self.slot(a, b, d)
        return pltpu.make_async_copy(self.terms.at[z, y, x, p.c], self.mine.at[n], self.load.at[n])

    def begin(self):
        for a, b, d in self.order():
            self.start("c", b, a, d)
            self.loading(a, b, d).start()

    def gathered(self, a, b, d):
        p = self.place
        self.loading(a, b, d).wait()
        self.arrived("c", b, a, d)
        n = self.slot(a, b, d)
        parts = [self.mine.at[n], self.r0.at[n]]
        if a == 0:
            for k in range(1, p.nx):
                self.arrived("t", k, b, d)
                parts.append(self.r1.at[self.slot(k - 1, b, d)])
            if b == 0:
                for k in range(1, p.nx):
                    self.arrived("s", k, d)
                    parts.append(self.r2.at[self.slot(0, k - 1, d)])
        return parts

    def add(self, target, parts):
        def step(slab, _):
            total = parts[0][slab].astype(F32)
            for part in parts[1:]:
                total = total + part[slab].astype(F32)
            target[slab] = total.astype(target.dtype)
            return 0

        lax.fori_loop(0, target.shape[0], step, 0)

    def steps(self):
        def step(a, b, d):
            def run():
                parts = self.gathered(a, b, d)
                if (a, b, d) == (0, 0, 0):
                    for k in range(1, self.place.nz):
                        self.arrived("z", k)
                        parts.append(self.r3.at[k - 1])
                    self.add(self.out, parts)
                    return
                self.add(parts[0], parts)
                if a:
                    self.start("t", a, b, d)
                elif b:
                    self.start("s", b, d)
                else:
                    self.start("z", d)

            return run

        return [step(a, b, d) for a, b, d in self.order()]


def semaphores(count, keys, locals_):
    return [
        pltpu.SemaphoreType.DMA((count, keys)),
        pltpu.SemaphoreType.DMA((count, keys)),
        pltpu.SemaphoreType.DMA((count, locals_)),
    ]


def split3(value):
    first = value.astype(BF16)
    rest = value - first.astype(F32)
    second = rest.astype(BF16)
    return first, second, (rest - second.astype(F32)).astype(BF16)


def to_rows(x_ref, m, cols, narrow):
    value = x_ref[:, m, cols].astype(F32).T
    return jnp.where(lane_index(value.shape) < narrow, value, 0.0)


def from_rows(out_ref, m, cols, value):
    out_ref[:, m, cols] = value.T.astype(out_ref.dtype)


def segment_of(lengths_ref, pad_ref, row, positions, seq):
    docs = lengths_ref.shape[1]
    end = 0
    counted = jnp.zeros_like(positions)
    for doc in range(docs):
        end = end + lengths_ref[row, doc]
        counted = counted + (end <= positions).astype(jnp.int32)
    return jnp.where(positions >= seq - pad_ref[0, row], docs + positions, counted)


def attention_masks(lengths_ref, pad_ref, row, bias_ref, qx_ref, kx_ref, block, transposed):
    docs = lengths_ref.shape[1]
    _, seq, lanes = qx_ref.shape
    head = lanes // 2
    down = segment_of(lengths_ref, pad_ref, row, lax.broadcasted_iota(jnp.int32, (seq, lanes), 0), seq)
    across = segment_of(lengths_ref, pad_ref, row, lax.broadcasted_iota(jnp.int32, (1, seq), 1), seq)
    r = lax.broadcasted_iota(jnp.int32, (block, block), 0)
    c = lax.broadcasted_iota(jnp.int32, (block, block), 1)
    causal = r <= c if transposed else c <= r
    for i in range(seq // block):
        part = slice(i * block, (i + 1) * block)
        same = jnp.concatenate([down[part]] * (block // lanes), axis=1) == across[:, part]
        bias_ref[i] = jnp.where(causal & same, 0.0, masked_score)
    lane = lane_index((seq, lanes))
    hot_at = jnp.minimum(down, docs)
    for h in range(2):
        spare = lane - (1 - h) * head
        used = (spare >= 0) & (spare <= docs)
        hot = hot_at == spare
        qx_ref[h] = jnp.where(used & ~hot, masked_score, 0.0).astype(BF16)
        ones = (spare > docs) & (spare <= docs + 3)
        kx_ref[h] = jnp.where((used & hot) | ones, 1.0, 0.0).astype(BF16)


def attention_forward(q, k, v, bias_ref, qx_ref, kx_ref, block, back, att_ref, lse_ref):
    seq, lanes = q.shape
    head = lanes // 2
    lane = lane_index((seq, lanes))
    q = q * jnp.asarray(head**-0.5, BF16)
    own = [lane < head, lane >= head]
    queries = [jnp.where(own[h], q, qx_ref[h]) for h in range(2)]
    keys = [jnp.where(own[h], k, kx_ref[h]) for h in range(2)]
    values = [jnp.where(own[h], v, jnp.asarray(1.0, BF16)) for h in range(2)]
    units = []
    for i in range(seq // block):
        for h in range(2):
            units.append((i, h, max(0, i - back) * block, i * block, (i + 1) * block))

    def scores(unit):
        i, h, low, start, stop = unit
        part = queries[h][start:stop]
        out = []
        if low < start:
            out.append(dot(part, keys[h][low:start], NT))
        out.append(dot(part, keys[h][start:stop], NT) + bias_ref[i])
        return out

    ahead = scores(units[0])
    for n, (i, h, low, start, stop) in enumerate(units):
        parts = ahead
        if n + 1 < len(units):
            ahead = scores(units[n + 1])
        top = functools.reduce(jnp.maximum, [jnp.max(p, axis=1, keepdims=True) for p in parts])
        probs = [jnp.exp(p - top).astype(BF16) for p in parts]
        out = dot(probs[-1], values[h][start:stop])
        if low < start:
            out = out + dot(probs[0], values[h][low:start])
        total = pltpu.roll(out, head, 1)
        result = (out / total, top + jnp.log(total))
        if h == 0:
            first = result
        else:
            left = lane[:block] < head
            att_ref[start:stop, :] = jnp.where(left, first[0], result[0]).astype(BF16)
            lse_ref[start:stop, :] = jnp.where(left, first[1], result[1])


def spread_vectors(packed, per, width):
    lanes = packed.shape[1]
    column = lane_index((lanes, width))
    owner = ((column.astype(F32) + 0.5) * (1.0 / per)).astype(jnp.int32)
    place = column - owner * per
    hot = jnp.where(place == lax.broadcasted_iota(jnp.int32, (lanes, width), 0), 1.0, 0.0).astype(BF16)
    spread = dot(packed, hot).reshape(-1, 8, width)
    shape = spread.shape
    column = lax.broadcasted_iota(jnp.int32, shape, 2)
    owner = ((column.astype(F32) + 0.5) * (1.0 / per)).astype(jnp.int32)
    return jnp.sum(jnp.where(owner == lax.broadcasted_iota(jnp.int32, shape, 0), spread, 0.0), axis=0)


FORWARD_TIMES = (
    ((1, 1, 1), (2, 2, 2, 2), (7, 7, 7, 7, 8, 8, 8, 8)),
    ((1, 2, 2), (4, 4, 4, 4), (11, 11, 11, 11, 12, 12, 12, 12)),
    ((3, 5, 6), (8, 8, 9, 9), (14, 14, 15, 15, 16, 16, 16, 16)),
)


def forward_times(plans, count):
    out = []
    for n, plan in enumerate(plans):
        nz, n2 = plan.place.nz, plan.place.nx
        items = plan.steps()
        start = 0
        for times, length in zip(FORWARD_TIMES[n], (nz - 1, nz * (n2 - 1), nz * n2 * (n2 - 1))):
            for m in range(length):
                at = times[m * len(times) // length]
                out.append((max(1, at * count // 16), items[start + m]))
            start += length
    out.sort(key=lambda entry: entry[0])
    return out


def tile_vectors(flat, per):
    length = flat.shape[1]
    vector_of = lambda f: jnp.minimum(((f.astype(F32) + 0.5) * (1.0 / per)).astype(jnp.int32), 6)
    f = lane_index((8, length))
    rows = jnp.where(vector_of(f) == lax.broadcasted_iota(jnp.int32, f.shape, 0), flat.astype(F32), 0.0)
    f = lax.broadcasted_iota(jnp.int32, (length, 128), 0)
    hot = jnp.where(f - vector_of(f) * per == lane_index(f.shape), 1.0, 0.0)
    return dot(rows.astype(BF16), hot.astype(BF16)).astype(BF16)


def forward_kernel(
    sizes, narrow, block, back, first_steps, per_ff,
    lengths_ref, pad_ref, x_ref, small_ref, wqkv_ref, wout_ref, wup_ref, wdown_ref,
    small_all, wqkv_all, wout_all, wup_all, wdown_all, vec_ref, bup_ref, normed_ref, qkv_ref, att_ref, lse_ref,
    send, recv, local, tile_s, small_s, wide_s, w_s, scaled_s, qkv_s, bias_s, qx_s, kx_s, load,
):
    step = pl.program_id(0)
    rows, seq, width = scaled_s.shape
    pairs = qkv_s.shape[0] // 3
    chunk = seq // first_steps
    place = Place(*sizes)
    ends = [
        (tile_s, small_all),
        (wqkv_ref, wqkv_all),
        (wout_ref, wout_all),
        (wup_ref, wup_all),
        (wdown_ref, wdown_all),
    ]
    plans = [Gather(place, s, f, send.at[n], recv.at[n], local.at[n, 0]) for n, (s, f) in enumerate(ends)]
    last = pl.num_programs(0) - 1
    count = first_steps + rows * pairs
    later = forward_times(plans[2:], count)

    @pl.when(step == 0)
    def _():
        place.greet()
        tile_s[0] = tile_vectors(small_ref[...], width // (small_all.shape[0] * small_all.shape[1] * small_all.shape[2] * 2))
        for plan in plans:
            plan.begin()
        for i in range(first_steps):
            for m in range(rows):
                cols = slice(i * chunk, (i + 1) * chunk)
                x = to_rows(x_ref, m, cols, narrow)
                whole = jnp.where(lane_index(x.shape) < narrow, x, -row_sum(x))
                scaled_s[m, cols, :] = whole * lax.rsqrt(row_sum(whole * whole) / width + epsilon)
        for one, two in zip(plans[0].steps(), plans[1].steps()):
            one()
            two()
        plans[0].landed()
        copy = pltpu.make_async_copy(small_all, small_s, load)
        copy.start()
        copy.wait()
        packed = small_s[...].astype(F32).reshape(-1, small_s.shape[-1]).astype(BF16)
        devices = packed.shape[0] // 8
        vec_ref[...] = spread_vectors(packed, width // devices, width)
        bup_ref[...] = spread_vectors(packed, per_ff, bup_ref.shape[1])
        plans[1].landed()
        copy = pltpu.make_async_copy(wqkv_all, wide_s, load)
        copy.start()
        copy.wait()
        for n in range(w_s.shape[1] // width):
            cols = slice(n * width, (n + 1) * width)
            w_s[:, cols] = wide_s[..., cols].astype(F32).reshape(-1, width).astype(BF16)

    for n in range(1, count):
        some = [item for at, item in later if at == n]
        if some:

            @pl.when(step == n)
            def _():
                for item in some:
                    item()

    @pl.when(step < first_steps)
    def _():
        cols = pl.ds(pl.multiple_of(step * chunk, chunk), chunk)
        normed = (scaled_s[:, cols, :].reshape(-1, width) * vec_ref[0:1, :]).astype(BF16)
        normed_ref[...] = normed.reshape(normed_ref.shape)
        for n in range(3):
            res = dot(normed, w_s[:, n * width : (n + 1) * width])
            if n != 1:
                res = res + vec_ref[1 + n // 2 : 2 + n // 2, :]
            res = res.astype(BF16)
            lanes = width // pairs
            for i in range(pairs):
                piece = res[:, i * lanes : (i + 1) * lanes].reshape(rows, chunk, lanes)
                qkv_s[n * pairs + i, :, cols, :] = piece
                qkv_ref[n * pairs + i] = piece

    @pl.when(step >= first_steps)
    def _():
        number = step - first_steps
        row = number // pairs
        pair = number % pairs

        @pl.when(pair == 0)
        def _():
            attention_masks(lengths_ref, pad_ref, row, bias_s, qx_s, kx_s, block, False)

        attention_forward(
            qkv_s[pair, row], qkv_s[pairs + pair, row], qkv_s[2 * pairs + pair, row],
            bias_s, qx_s, kx_s, block, back, att_ref, lse_ref,
        )

    @pl.when(step == last)
    def _():
        for at, item in later:
            if at >= count:
                item()
        for plan in plans[2:]:
            plan.landed()
        for plan in plans:
            plan.sent()


def forward(sizes, lengths, pad_len, x, small, matrices, per_ff, block=256, first_steps=4):
    narrow, rows, seq = x.shape
    width = narrow + 1
    pairs = HEADS // 2
    lanes = width // pairs
    nz, ny, nx = sizes
    devices = nz * ny * nx * 2
    ff = per_ff * devices
    back = -(-(MOST - 1) // block)
    chunk = seq // first_steps
    packed = jax.ShapeDtypeStruct((1, 8, 128), BF16)
    shards = [packed] + [m.reshape(-1, 8, m.shape[1]) for m in matrices]
    every = pl.BlockSpec(memory_space=pl.ANY)
    smem = pl.BlockSpec(memory_space=pltpu.SMEM)
    fixed = lambda *shape: pl.BlockSpec(shape, lambda s: (0,) * len(shape))
    early = lambda s: jnp.minimum(s, first_steps - 1)
    number = lambda s: jnp.maximum(s - first_steps, 0)
    head_pair = pl.BlockSpec((None, None, seq, lanes), lambda s: (number(s) % pairs, number(s) // pairs, 0, 0))
    wide = matrices[0].shape[1]
    outs = pl.pallas_call(
        functools.partial(forward_kernel, sizes, narrow, block, back, first_steps, per_ff),
        grid=(first_steps + rows * pairs,),
        in_specs=[smem, smem, pl.BlockSpec((width, rows, seq), lambda s: (0, 0, 0), pipeline_mode=pl.Buffered(1))]
        + [fixed(*small.shape)]
        + [every] * 4,
        out_specs=[every] * 5
        + [
            fixed(8, width),
            fixed(8, ff),
            pl.BlockSpec((rows, chunk, width), lambda s: (0, early(s), 0)),
            pl.BlockSpec((3 * pairs, rows, chunk, lanes), lambda s: (0, 0, early(s), 0)),
            head_pair,
            head_pair,
        ],
        out_shape=[jax.ShapeDtypeStruct((nz, ny, nx, 2) + s.shape, BF16) for s in shards]
        + [
            jax.ShapeDtypeStruct((8, width), F32),
            jax.ShapeDtypeStruct((8, ff), F32),
            jax.ShapeDtypeStruct((rows, seq, width), BF16),
            jax.ShapeDtypeStruct((3 * pairs, rows, seq, lanes), BF16),
            jax.ShapeDtypeStruct((pairs, rows, seq, lanes), BF16),
            jax.ShapeDtypeStruct((pairs, rows, seq, lanes), F32),
        ],
        scratch_shapes=semaphores(5, len(Gather.keys(nz, nx)), 1)
        + [
            pltpu.VMEM(packed.shape, BF16),
            pltpu.VMEM((nz, ny, nx, 2) + packed.shape, BF16),
            pltpu.VMEM((nz, ny, nx, 2) + shards[1].shape, BF16),
            pltpu.VMEM((width, wide), BF16),
            pltpu.VMEM((rows, seq, width), F32),
            pltpu.VMEM((3 * pairs, rows, seq, lanes), BF16),
            pltpu.VMEM((seq // block, block, block), F32),
            pltpu.VMEM((2, seq, lanes), BF16),
            pltpu.VMEM((2, seq, lanes), BF16),
            pltpu.SemaphoreType.DMA,
        ],
        compiler_params=pltpu.CompilerParams(
            collective_id=1, has_side_effects=True, vmem_limit_bytes=vmem_grant
        ),
        name="forward",
    )(lengths, pad_len, x, small, *shards[1:])
    large = [w.reshape(-1, m.shape[1]) for w, m in zip(outs[1:5], matrices)]
    return large, outs[5:]


def norm_back(d_normed, scaled, factor, gain, width):
    grad_gain = jnp.sum(d_normed * scaled, axis=0, keepdims=True)
    e = d_normed * gain
    d_whole = factor * (e - scaled * (row_sum(e * scaled) / width))
    last = row_sum(jnp.where(lane_index(d_whole.shape) == width - 1, d_whole, 0.0))
    return grad_gain, d_whole, last


def token_block(x_ref, narrow):
    _, rows, chunk = x_ref.shape
    return jnp.concatenate([to_rows(x_ref, m, slice(0, chunk), narrow) for m in range(rows)], axis=0)


def put_block(out_ref, value):
    _, rows, chunk = out_ref.shape
    for m in range(rows):
        from_rows(out_ref, m, slice(0, chunk), value[m * chunk : (m + 1) * chunk])


def beside(ref):
    pieces, rows, chunk, lanes = ref.shape
    return jnp.concatenate([ref[i].reshape(rows * chunk, lanes) for i in range(pieces)], axis=1)


def keep_pieces(ref, start, value):
    lanes = ref.shape[3]
    for i in range(value.shape[1] // lanes):
        piece = value[:, i * lanes : (i + 1) * lanes]
        ref[start // lanes + i] = piece.reshape(ref.shape[1:])


def mlp_kernel(
    narrow, slab,
    x_ref, cot_ref, att_ref, w_out_ref, w_up_ref, w_down_ref, vec_ref, bup_ref,
    out_ref, act_ref, dh_ref, n2_ref, d2_ref, df_ref, dmid_ref, datt_ref, sums_ref, gbu_ref,
):
    width, rows, chunk = x_ref.shape
    ff = w_up_ref.shape[1]
    tokens = rows * chunk
    inside = lane_index((tokens, width)) < narrow
    b_out, gain, b_down = vec_ref[3:4, :], vec_ref[4:5, :], vec_ref[5:6, :]

    @pl.when(pl.program_id(0) == 0)
    def _():
        sums_ref[...] = jnp.zeros_like(sums_ref)
        gbu_ref[...] = jnp.zeros_like(gbu_ref)

    def keep(ref, cols, value):
        ref[:, :, cols] = value.reshape(rows, chunk, -1)

    every = slice(0, width)
    branch = dot(beside(att_ref), w_out_ref[...]) + b_out
    up = token_block(cot_ref, narrow)
    d2 = up - row_sum(up) / width
    grad_b_down = jnp.sum(d2, axis=0, keepdims=True)
    d2 = d2.astype(BF16)
    keep(d2_ref, every, d2)
    branch = branch - row_sum(branch) / width
    middle = jnp.where(inside, token_block(x_ref, narrow) + branch, 0.0)
    whole = jnp.where(inside, middle, -row_sum(middle))
    factor = lax.rsqrt(row_sum(whole * whole) / width + epsilon)
    scaled = whole * factor
    n2 = (scaled * gain).astype(BF16)
    keep(n2_ref, every, n2)

    def stage(n):
        cols = slice(n * slab, (n + 1) * slab)
        return dot(n2, w_up_ref[:, cols]), dot(d2, w_down_ref[cols, :], NT)

    count = ff // slab
    ahead = stage(0)
    for n in range(count):
        cols = slice(n * slab, (n + 1) * slab)
        hidden, d_act = ahead
        if n + 1 < count:
            ahead = stage(n + 1)
        hidden = hidden + bup_ref[6:7, cols]
        square = hidden * hidden
        half = 0.5 + 0.5 * jnp.tanh(hidden * (gelu_c0 + gelu_c1 * square))
        active = hidden * half
        slope = half + active * (1.0 - half) * (2.0 * gelu_c0 + (6.0 * gelu_c1) * square)
        keep_pieces(act_ref, n * slab, active.astype(BF16))
        d_hidden = d_act * slope
        gbu_ref[:, cols] += jnp.sum(d_hidden, axis=0, keepdims=True)
        keep_pieces(dh_ref, n * slab, d_hidden.astype(BF16))
    dn2 = dot(beside(dh_ref), w_up_ref[...], NT)
    b2 = dot(beside(act_ref), w_down_ref[...]) + b_down
    grad_gain, d_whole, last = norm_back(dn2, scaled, factor, gain, width)
    d_mid = jnp.where(inside, up + d_whole - last, 0.0)
    dmid_ref[...] = d_mid.reshape(dmid_ref.shape)
    d_first = d_mid - row_sum(d_mid) / width
    sums_ref[3:4, :] += jnp.sum(d_first, axis=0, keepdims=True)
    sums_ref[4:5, :] += grad_gain
    sums_ref[5:6, :] += grad_b_down
    d_first = d_first.astype(BF16)
    keep(df_ref, every, d_first)
    keep_pieces(datt_ref, 0, dot(d_first, w_out_ref[...], NT).astype(BF16))
    put_block(out_ref, middle + b2 - row_sum(b2) / width)


def mlp(x, cot, att, w_out, w_up, w_down, vectors, b_up, chunk=256, slab=1024, tile=512):
    narrow, rows, seq = x.shape
    width = narrow + 1
    ff = w_up.shape[1]
    per_token = lambda n: pl.BlockSpec((rows, chunk, n), lambda i: (0, i, 0))
    pieces = lambda like: pl.BlockSpec(like.shape[:2] + (chunk,) + like.shape[3:], lambda i: (0, 0, i, 0))
    split = jax.ShapeDtypeStruct((ff // tile, rows, seq, tile), BF16)
    feature_first = pl.BlockSpec((width, rows, chunk), lambda i: (0, 0, i))
    fixed = lambda *shape: pl.BlockSpec(shape, lambda i: (0, 0))
    once = lambda *shape: pl.BlockSpec(shape, lambda i: (0, 0), pipeline_mode=pl.Buffered(1))
    tokens = lambda n, dtype: jax.ShapeDtypeStruct((rows, seq, n), dtype)
    return pl.pallas_call(
        functools.partial(mlp_kernel, narrow, slab),
        grid=(seq // chunk,),
        in_specs=[feature_first, feature_first, pieces(att)]
        + [once(width, width), once(width, ff), once(ff, width), once(8, width), once(8, ff)],
        out_specs=[feature_first, pieces(split), pieces(split)]
        + [per_token(width)] * 4
        + [pieces(att)]
        + [fixed(8, width), fixed(1, ff)],
        out_shape=[
            jax.ShapeDtypeStruct(x.shape, BF16),
            split,
            split,
            tokens(width, BF16),
            tokens(width, BF16),
            tokens(width, BF16),
            tokens(width, F32),
            jax.ShapeDtypeStruct(att.shape, BF16),
            jax.ShapeDtypeStruct((8, width), F32),
            jax.ShapeDtypeStruct((1, ff), F32),
        ],
        compiler_params=pltpu.CompilerParams(vmem_limit_bytes=vmem_grant),
        name="mlp",
    )(x, cot, att, w_out, w_up, w_down, vectors, b_up)


def attention_backward(
    docs, q, k, v, att, d_att, lse, bias_ref, qx_ref, kx_ref, dq_s, block, back, dq_ref, dk_ref, dv_ref
):
    seq, lanes = q.shape
    head = lanes // 2
    lane = lane_index((seq, lanes))
    q = q * jnp.asarray(head**-0.5, BF16)
    product = d_att.astype(F32) * att.astype(F32)
    high = product.astype(BF16)
    low = (product - high.astype(F32)).astype(BF16)
    r = lax.broadcasted_iota(jnp.int32, (lanes, lanes), 0)
    c = lax.broadcasted_iota(jnp.int32, (lanes, lanes), 1)
    swap = jnp.where((r < head) != (c < head), 1.0, 0.0).astype(BF16)
    delta = split3(-(dot(high, swap) + dot(low, swap)))
    minus_lse = split3(-pltpu.roll(lse, head, 1))
    own = [lane < head, lane >= head]
    queries, keys, values, upstream = [], [], [], []
    for h in range(2):
        spare = lane - (1 - h) * head
        qx = qx_ref[h]
        dx = jnp.zeros_like(d_att)
        for n in range(3):
            qx = jnp.where(spare == docs + 1 + n, minus_lse[n], qx)
            dx = jnp.where(spare == n, delta[n], dx)
        vx = jnp.where((spare >= 0) & (spare < 3), 1.0, 0.0).astype(BF16)
        queries.append(jnp.where(own[h], q, qx))
        keys.append(jnp.where(own[h], k, kx_ref[h]))
        values.append(jnp.where(own[h], v, vx))
        upstream.append(jnp.where(own[h], d_att, dx))
        dq_s[h] = jnp.zeros((seq, lanes), F32)
    units = []
    for j in range(seq // block):
        for h in range(2):
            units.append((j, h, j * block, (j + 1) * block, min(seq, (j + 1 + back) * block)))

    def products(unit):
        _, h, start, stop, top = unit
        return (
            dot(keys[h][start:stop], queries[h][start:top], NT),
            dot(values[h][start:stop], upstream[h][start:top], NT),
        )

    left = lane[:block] < head
    sum_values = jnp.zeros((1, lanes), F32)
    ahead = products(units[0])
    for n, (j, h, start, stop, top) in enumerate(units):
        scores, d_probs = ahead
        if n + 1 < len(units):
            ahead = products(units[n + 1])
        near = scores[:, :block] + bias_ref[j]
        scores = jnp.concatenate([near, scores[:, block:]], axis=1) if top > stop else near
        probs = jnp.exp(scores)
        d_scores = (probs * d_probs).astype(BF16)
        d_values = dot(probs.astype(BF16), d_att[start:top])
        d_keys = dot(d_scores, q[start:top])
        dq_s[h, start:top, :] += dot(d_scores, k[start:stop], TN)
        if h == 0:
            first = (d_values, d_keys)
        else:
            d_values = jnp.where(left, first[0], d_values)
            sum_values = sum_values + jnp.sum(d_values, axis=0, keepdims=True)
            dv_ref[start:stop, :] = d_values.astype(BF16)
            dk_ref[start:stop, :] = jnp.where(left, first[1], d_keys).astype(BF16)
    d_query = jnp.where(lane < head, dq_s[0], dq_s[1]) * head**-0.5
    dq_ref[...] = d_query.astype(BF16)
    return jnp.sum(d_query, axis=0, keepdims=True), sum_values


class Sums(Scatter):
    @staticmethod
    def buffers(nz, n2, block, dtype):
        return Scatter.buffers(nz, n2, block, dtype)[1:]

    def __init__(self, place, terms, out, buffers, send, recv):
        Transfer.__init__(self, place, send, recv)
        self.terms, self.out = terms, out
        self.r0, self.r1, self.r2, self.r3 = buffers
        self.slabs = out.shape[0]

    def term(self, a, b, d, other_core=False):
        p = self.place
        wide, narrow = p.device(a, b, d, other_core)
        device = wide * (p.nx * 2) + narrow
        return self.terms.at[pl.ds(device * self.slabs, self.slabs)]

    def ends(self, key):
        p = self.place
        kind = key[0]
        if kind == "c":
            a, b, d = key[1:]
            return self.term(a, b, d, True), self.r0.at[self.slot(b, a, d)], p.device(0, 0, 0, True)
        if kind == "t":
            a, b, d = key[1:]
            return self.term(a, b, d), self.r1.at[self.slot(a - 1, b, d)], p.device(a, 0, 0)
        if kind == "s":
            b, d = key[1:]
            return self.term(0, b, d), self.r2.at[self.slot(0, b - 1, d)], p.device(0, b, 0)
        return self.term(0, 0, key[1]), self.r3.at[key[1] - 1], p.device(0, 0, key[1])

    def begin(self):
        for a, b, d in self.order():
            self.start("c", b, a, d)

    def gathered(self, a, b, d):
        p = self.place
        self.arrived("c", b, a, d)
        parts = [self.term(a, b, d), self.r0.at[self.slot(a, b, d)]]
        if a == 0:
            for k in range(1, p.nx):
                self.arrived("t", k, b, d)
                parts.append(self.r1.at[self.slot(k - 1, b, d)])
            if b == 0:
                for k in range(1, p.nx):
                    self.arrived("s", k, d)
                    parts.append(self.r2.at[self.slot(0, k - 1, d)])
        return parts


def as_slabs(value):
    return value.reshape(-1, 8, value.shape[1]).astype(BF16)


def backward_times(tiles, steps, per_chunk):
    a = 2 * tiles + 1
    spread = lambda start, stop, n: [start + (stop - start) * i // n for i in range(n)]
    return [
        (tiles, spread(tiles + 1, 2 * tiles - 2, 8), spread(2 * tiles, a + 2, 4), spread(a + 2, a + 4, 3), a + 7),
        (2 * tiles, spread(2 * tiles + 1, a + 4, 8), spread(a + 5, a + 7, 4), spread(a + 7, a + 9, 3), steps),
        (a, spread(a + 3, a + 5, 8), spread(a + 6, a + 7, 4), spread(a + 8, a + 9, 3), a + 10),
        (a + per_chunk, spread(a + per_chunk + 1, a + per_chunk + 3, 8), [a + 8] * 4, [a + 9] * 3, a + 11),
        (a + 2 * per_chunk, [a + 2 * per_chunk + 1] * 8, [a + 10] * 4, [a + 11] * 3, steps),
    ]


def stage_steps(plan, times):
    nz, n2 = plan.place.nz, plan.place.nx
    counts = (nz * n2 * (n2 - 1), nz * (n2 - 1), nz - 1, 1)
    items = plan.steps()
    due = []
    for stage, count in zip(times[1:], counts):
        stage = stage if isinstance(stage, list) else [stage]
        due += [stage[m * len(stage) // count] for m in range(count)]
    return list(zip(due, items))


def backward_kernel(
    sizes, block, back, tiles, chunks,
    lengths_ref, pad_ref, act_ref, dh_ref, d2_ref, n2_ref, att_all, df_ref, n1_ref,
    q_ref, k_ref, v_ref, att_ref, datt_ref, lse_ref,
    dq_out, dk_out, dv_out, sq_ref, sv_ref, left_ref, *refs,
):
    kept = chunks - 1
    count = 3 + kept
    outs, refs = refs[:count], refs[count:]
    send, recv, bias_s, qx_s, kx_s, dq_s, pair_s, x_s, y_s, z_s, load = refs[:11]
    terms, bufs = refs[11 : 11 + count], refs[11 + count :]
    step = pl.program_id(0)
    rows, seq, width = x_s.shape
    tokens = rows * seq
    place = Place(*sizes)
    plans = [
        Sums(place, terms[n], outs[n], bufs[4 * n : 4 * n + 4], send.at[n], recv.at[n]) for n in range(count)
    ]
    first = 2 * tiles + 1
    pairs = (3 * width) // (3 * q_ref.shape[1])
    per_chunk = rows * pairs // chunks
    steps = first + rows * pairs
    times = backward_times(tiles, steps, per_chunk)
    due = []
    for n, plan in enumerate(plans):
        due.append((times[n][0], plan.begin))
        due += stage_steps(plan, times[n])
    flat = lambda ref: ref[...].reshape(tokens, -1)
    fetch = lambda source, target, n: pltpu.make_async_copy(source, target, load.at[n])

    @pl.when(step == 0)
    def _():
        place.greet()
        fetch(d2_ref, x_s, 0).start()
        fetch(n2_ref, y_s, 1).start()
        fetch(att_all, z_s, 2).start()
        fetch(d2_ref, x_s, 0).wait()

    @pl.when(step == tiles)
    def _():
        fetch(df_ref, x_s, 0).start()
        fetch(n2_ref, y_s, 1).wait()

    @pl.when(step == 2 * tiles)
    def _():
        fetch(n1_ref, y_s, 1).start()
        fetch(att_all, z_s, 2).wait()
        fetch(df_ref, x_s, 0).wait()

    @pl.when(step == first)
    def _():
        fetch(n1_ref, y_s, 1).wait()

    for n in range(steps):
        some = [item for at, item in due if at == n]
        if some:

            @pl.when(step == n)
            def _():
                for item in some:
                    item()

    @pl.when(step < tiles)
    def _():
        tile = as_slabs(dot(flat(act_ref), flat(x_s), TN))
        terms[0][pl.ds(step * tile.shape[0], tile.shape[0])] = tile

    @pl.when((step >= tiles) & (step < 2 * tiles))
    def _():
        tile = as_slabs(dot(flat(y_s), flat(dh_ref), TN))
        lanes = tile.shape[2]
        terms[1][:, :, pl.ds(pl.multiple_of((step - tiles) * lanes, lanes), lanes)] = tile

    @pl.when(step == 2 * tiles)
    def _():
        terms[2][...] = as_slabs(dot(beside(z_s), flat(x_s), TN))

    @pl.when(step >= first)
    def _():
        number = step - first
        row = number % rows
        lanes = q_ref.shape[1]

        @pl.when(number < rows)
        def _():
            attention_masks(lengths_ref, pad_ref, row, bias_s.at[row], qx_s.at[row], kx_s.at[row], block, True)

        sum_query, sum_values = attention_backward(
            lengths_ref.shape[1], q_ref[...], k_ref[...], v_ref[...], att_ref[...], datt_ref[...], lse_ref[...],
            bias_s.at[row], qx_s.at[row], kx_s.at[row], dq_s, block, back,
            pair_s.at[0, row], pair_s.at[1, row], pair_s.at[2, row],
        )
        for n, ref in enumerate((dq_out, dk_out, dv_out)):
            ref[...] = pair_s[n, row]

        @pl.when(row == 0)
        def _():
            sq_ref[...] = sum_query
            sv_ref[...] = sum_values

        @pl.when(row > 0)
        def _():
            sq_ref[...] += sum_query
            sv_ref[...] += sum_values

    per = pairs // chunks
    for pair in range(pairs):

        @pl.when(step == first + rows * pair + rows - 1)
        def _():
            lanes = q_ref.shape[1]
            right = jnp.concatenate([pair_s[n].reshape(tokens, lanes) for n in range(3)], axis=1)
            tile = as_slabs(dot(flat(y_s), right, TN))
            target = terms[3 + pair // per] if pair // per < kept else left_ref
            target[:, :, (pair % per) * 3 * lanes : (pair % per + 1) * 3 * lanes] = tile

    @pl.when(step == steps - 1)
    def _():
        for at, item in due:
            if at >= steps:
                item()
        for plan in plans:
            plan.sent()


def backward(
    sizes, lengths, pad_len, active, d_hidden, d_second, normed_second, attended, d_first, normed_first, qkv, d_attended,
    log_sums, block=256, chunks=3,
):
    nz, ny, nx = sizes
    pairs, rows, seq, lanes = attended.shape
    width = pairs * lanes
    tiles, tile = active.shape[0], active.shape[3]
    ff = tiles * tile
    devices = nz * ny * nx * 2
    back = -(-(MOST - 1) // block)
    first = 2 * tiles + 1
    steps = first + rows * pairs
    every = pl.BlockSpec(memory_space=pl.ANY)
    smem = pl.BlockSpec(memory_space=pltpu.SMEM)
    number = lambda s: jnp.maximum(s - first, 0)
    head_pair = pl.BlockSpec((None, None, seq, lanes), lambda s: (number(s) // rows, number(s) % rows, 0, 0))
    kind = lambda n: pl.BlockSpec((None, None, seq, lanes), lambda s: (n * pairs + number(s) // rows, number(s) % rows, 0, 0))
    sums = pl.BlockSpec((1, lanes), lambda s: (0, number(s) // rows))
    part = [(ff, width), (width, ff), (width, width)] + [(width, 3 * width // chunks)] * (chunks - 1)
    blocks = [(m // devices // 8, 8, n) for m, n in part]
    left = (width // 8, 8, 3 * width // chunks)
    fixed = lambda shape: pl.BlockSpec(shape, lambda s: (0,) * len(shape), pipeline_mode=pl.Buffered(1))
    bufs = []
    for b in blocks:
        bufs += Sums.buffers(nz, nx, b, BF16)
    keys = len(Scatter.keys(nz, nx))
    token = jax.ShapeDtypeStruct(attended.shape, BF16)
    held = pltpu.VMEM((rows, seq, width), BF16)
    outs = pl.pallas_call(
        functools.partial(backward_kernel, sizes, block, back, tiles, chunks),
        grid=(steps,),
        in_specs=[
            smem,
            smem,
            pl.BlockSpec((None, rows, seq, tile), lambda s: (jnp.minimum(s, tiles - 1), 0, 0, 0)),
            pl.BlockSpec((None, rows, seq, tile), lambda s: (jnp.clip(s - tiles, 0, tiles - 1), 0, 0, 0)),
        ]
        + [every] * 5
        + [kind(0), kind(1), kind(2), head_pair, head_pair, head_pair],
        out_specs=[head_pair, head_pair, head_pair, sums, sums, fixed(left)] + [fixed(b) for b in blocks],
        out_shape=[token, token, token]
        + [jax.ShapeDtypeStruct((1, width), F32)] * 2
        + [jax.ShapeDtypeStruct(left, BF16)]
        + [jax.ShapeDtypeStruct(b, F32) for b in blocks],
        scratch_shapes=semaphores(len(blocks), keys, 1)[:2]
        + [
            pltpu.VMEM((rows, seq // block, block, block), F32),
            pltpu.VMEM((rows, 2, seq, lanes), BF16),
            pltpu.VMEM((rows, 2, seq, lanes), BF16),
            pltpu.VMEM((2, seq, lanes), F32),
            pltpu.VMEM((3, rows, seq, lanes), BF16),
            held,
            held,
            pltpu.VMEM(attended.shape, BF16),
            pltpu.SemaphoreType.DMA((3,)),
        ]
        + [pltpu.VMEM((b[0] * devices,) + b[1:], BF16) for b in blocks]
        + bufs,
        compiler_params=pltpu.CompilerParams(
            collective_id=2, has_side_effects=True, vmem_limit_bytes=62 << 20
        ),
        name="backward",
    )(
        lengths, pad_len, active, d_hidden, d_second, normed_second, attended, d_first, normed_first,
        qkv, qkv, qkv, attended, d_attended, log_sums,
    )
    return outs


def collect_vectors(whole, per, lanes):
    width = whole.shape[1]
    devices = width // per
    column = lax.broadcasted_iota(jnp.int32, (devices, 8, width), 2)
    owner = ((column.astype(F32) + 0.5) * (1.0 / per)).astype(jnp.int32)
    device = lax.broadcasted_iota(jnp.int32, (devices, 8, width), 0)
    masked = jnp.where(owner == device, whole[None], 0.0).reshape(devices * 8, width)
    row = lax.broadcasted_iota(jnp.int32, (width, lanes), 0)
    place = row - ((row.astype(F32) + 0.5) * (1.0 / per)).astype(jnp.int32) * per
    hot = jnp.where(place == lane_index((width, lanes)), 1.0, 0.0).astype(BF16)
    return sum(dot(part, hot) for part in split3(masked)).reshape(devices, 8, lanes)


def back_kernel(
    sizes, narrow, per, per_ff,
    x_ref, dq_ref, dk_ref, dv_ref, w_ref, vec_ref, dmid_ref, sums_ref, sq_ref, sv_ref, gbu_ref, left_ref, *refs,
):
    count = len(refs) - 3 - 9 - 8
    done, refs = refs[:count], refs[count:]
    out_ref, wqkv_out, small_out = refs[:3]
    send, recv, small_send, small_recv, load, terms, total, small_terms, small_total = refs[3:12]
    bufs = refs[12:]
    step = pl.program_id(0)
    width, rows, chunk = x_ref.shape
    tokens = rows * chunk
    place = Place(*sizes)
    plan = Sums(place, terms, total, bufs[:4], send, recv)
    small = Sums(place, small_terms, small_total, bufs[4:], small_send, small_recv)
    fetch = pltpu.make_async_copy(left_ref, terms, load)
    grouped = []
    for one, two in zip(plan.steps(), small.steps()):
        grouped += [one, two]
    n2, nz = place.nx, place.nz
    ends = [0, 2 * nz * n2 * (n2 - 1), 2 * nz * n2 * n2 - 2 * nz, 2 * nz * n2 * n2 - 2, len(grouped)]

    @pl.when(step == 0)
    def _():
        fetch.start()
        place.greet()
        row = lax.broadcasted_iota(jnp.int32, sums_ref.shape, 0)
        whole = sums_ref[...] + jnp.where(row == 1, sq_ref[...], 0.0) + jnp.where(row == 2, sv_ref[...], 0.0)
        fetch.wait()
        plan.begin()
        pieces = collect_vectors(whole, per, small_terms.shape[2])
        row = lax.broadcasted_iota(jnp.int32, (8, gbu_ref.shape[1]), 0)
        pieces = pieces + collect_vectors(jnp.where(row == 6, gbu_ref[...], 0.0), per_ff, small_terms.shape[2])
        small_terms[...] = pieces
        small.begin()

    for n in range(3):

        @pl.when(step == n)
        def _():
            for item in grouped[ends[n] : ends[n + 1]]:
                item()

    dn = sum(
        dot(beside(ref), w_ref[:, n * width : (n + 1) * width], NT)
        for n, ref in enumerate((dq_ref, dk_ref, dv_ref))
    )
    x = token_block(x_ref, narrow)
    inside = lane_index(x.shape) < narrow
    whole = jnp.where(inside, x, -row_sum(x))
    factor = lax.rsqrt(row_sum(whole * whole) / width + epsilon)
    _, d_whole, last = norm_back(dn, whole * factor, factor, vec_ref[0:1, :], width)
    out_ref[...] = (dmid_ref[...].reshape(tokens, width) + d_whole - last).astype(BF16).reshape(out_ref.shape)

    @pl.when(step == pl.num_programs(0) - 1)
    def _():
        for item in grouped[ends[3] :]:
            item()
        chunks = list(done) + [total]
        lanes = 2 * (width // HEADS)
        pairs = chunks[0].shape[2] // (3 * lanes)
        for c, source in enumerate(chunks):
            for p in range(pairs):
                for n in range(3):
                    at = n * width + (c * pairs + p) * lanes
                    start = (p * 3 + n) * lanes
                    wqkv_out[:, :, at : at + lanes] = source[:, :, start : start + lanes]
        small_out[...] = small_total[0]
        plan.sent()
        small.sent()


def back(sizes, x, dq, dk, dv, w_qkv, vectors, dmid, sums, sq, sv, gbu, left, done, chunk=256):
    nz, ny, nx = sizes
    narrow, rows, seq = x.shape
    width = narrow + 1
    devices = nz * ny * nx * 2
    ff = gbu.shape[1]
    per, per_ff = width // devices, ff // devices
    per_token = pl.BlockSpec((rows, chunk, width), lambda i: (0, i, 0))
    feature_first = pl.BlockSpec((width, rows, chunk), lambda i: (0, 0, i))
    fixed = lambda shape: pl.BlockSpec(shape, lambda i: (0,) * len(shape), pipeline_mode=pl.Buffered(1))
    keys = len(Scatter.keys(nz, nx))
    block = (left.shape[0] // devices,) + left.shape[1:]
    slab = (block[0], 8, 3 * width)
    return pl.pallas_call(
        functools.partial(back_kernel, sizes, narrow, per, per_ff),
        grid=(seq // chunk,),
        in_specs=[feature_first]
        + [pl.BlockSpec(dq.shape[:2] + (chunk,) + dq.shape[3:], lambda i: (0, 0, i, 0))] * 3
        + [fixed((width, 3 * width)), fixed((8, width)), per_token]
        + [fixed((8, width)), fixed((1, width)), fixed((1, width)), fixed((1, ff)), pl.BlockSpec(memory_space=pl.ANY)]
        + [fixed(d.shape) for d in done],
        out_specs=[per_token, fixed(slab), fixed((8, 128))],
        out_shape=[
            jax.ShapeDtypeStruct((rows, seq, width), BF16),
            jax.ShapeDtypeStruct(slab, F32),
            jax.ShapeDtypeStruct((8, 128), F32),
        ],
        scratch_shapes=[pltpu.SemaphoreType.DMA((keys,))] * 4
        + [
            pltpu.SemaphoreType.DMA,
            pltpu.VMEM(left.shape, BF16),
            pltpu.VMEM(block, F32),
            pltpu.VMEM((devices, 8, 128), F32),
            pltpu.VMEM((1, 8, 128), F32),
        ]
        + Sums.buffers(nz, nx, block, BF16)
        + Sums.buffers(nz, nx, (1, 8, 128), F32),
        compiler_params=pltpu.CompilerParams(
            collective_id=3, has_side_effects=True, vmem_limit_bytes=vmem_grant
        ),
        name="back",
    )(x, dq, dk, dv, w_qkv, vectors, dmid, sums, sq, sv, gbu, left, *done)


def finish_kernel(small_ref, wqkv_ref, own_ref, gain_ref, x_ref, *refs):
    count = (len(refs) - 8) // 2
    shards, out_ref, wqkv_out, gain_out = refs[:count], refs[count], refs[count + 1], refs[count + 2]
    outs, smalls = refs[count + 3 : 2 * count + 3], refs[2 * count + 3 :]
    rows = x_ref.shape[0]
    for m in range(rows):
        from_rows(out_ref, m, slice(0, x_ref.shape[1]), x_ref[m].astype(F32))

    @pl.when(pl.program_id(0) == 0)
    def _():
        grad = wqkv_ref[...].reshape(wqkv_out.shape)
        wqkv_out[...] = grad
        total = jnp.broadcast_to(row_sum(grad * own_ref[...].astype(F32)), (grad.shape[0], 128)).T
        gain_out[...] = total[0:1, : gain_ref.shape[1]] / gain_ref[...].astype(F32)
        for source, target in zip(shards, outs):
            target[...] = source[...].reshape(target.shape)
        for n, target in enumerate(smalls):
            target[...] = small_ref[n + 1 : n + 2, : target.shape[1]]


def finish(small, grad_qkv, w_qkv, gain, grad_x, shards, lengths, narrow, chunk=256):
    rows, seq, width = grad_x.shape
    fixed = lambda shape: pl.BlockSpec(shape, lambda i: (0,) * len(shape), pipeline_mode=pl.Buffered(1))
    flat = lambda s: (s.shape[0] * 8, s.shape[2])
    shapes = [w_qkv.shape, (1, w_qkv.shape[0])] + [flat(s) for s in shards] + [(1, n) for n in lengths]
    operands = [small, grad_qkv, w_qkv, gain]
    return pl.pallas_call(
        finish_kernel,
        grid=(seq // chunk,),
        in_specs=[fixed(v.shape) for v in operands]
        + [pl.BlockSpec((rows, chunk, width), lambda i: (0, i, 0))]
        + [fixed(s.shape) for s in shards],
        out_specs=[pl.BlockSpec((width, rows, chunk), lambda i: (0, 0, i))] + [fixed(s) for s in shapes],
        out_shape=[jax.ShapeDtypeStruct((narrow, rows, seq), BF16)] + [jax.ShapeDtypeStruct(s, F32) for s in shapes],
        compiler_params=pltpu.CompilerParams(vmem_limit_bytes=vmem_grant),
        name="finish",
    )(*operands, grad_x, *shards)


def body(
    sizes,
    resid, lengths, pad_len, gain_attn, w_qkv, b_query, b_value, w_out, b_out, gain_mlp, w_up, b_up, w_down, b_down,
    cotangent,
):
    narrow = resid.shape[3]
    seq = resid.shape[2]
    docs = lengths.shape[2]
    lengths = lengths.reshape(-1, docs)
    pad_len = pad_len.reshape(1, -1)
    x = jnp.transpose(resid.reshape(-1, seq, narrow), (2, 0, 1))
    cot = jnp.transpose(cotangent.reshape(-1, seq, narrow), (2, 0, 1))
    small = [v.reshape(1, -1) for v in (gain_attn, b_query, b_value, b_out, gain_mlp, b_down, b_up)]
    small = jnp.concatenate(small, axis=1)
    small = jnp.pad(small, ((0, 0), (0, -small.shape[1] % 128)))
    large, (vectors, all_b_up, normed_first, qkv, attended, log_sums) = forward(
        sizes, lengths, pad_len, x, small, [w_qkv, w_out, w_up, w_down], b_up.shape[0]
    )
    all_qkv, all_out, all_up, all_down = large
    result, active, d_hidden, normed_second, d_second, d_first, d_middle, d_attended, sums, sum_b_up = mlp(
        x, cot, attended, all_out, all_up, all_down, vectors, all_b_up
    )
    d_query, d_keys, d_values, sum_query, sum_values, left, *shards = backward(
        sizes, lengths, pad_len, active, d_hidden, d_second, normed_second, attended, d_first, normed_first, qkv,
        d_attended, log_sums,
    )
    grad_tokens, grad_qkv, grad_small = back(
        sizes, x, d_query, d_keys, d_values, all_qkv, vectors, d_middle, sums, sum_query, sum_values, sum_b_up, left,
        shards[3:],
    )
    lengths = [v.shape[0] for v in (b_query, b_value, b_out, gain_mlp, b_down, b_up)]
    grad_x, grad_w_qkv, *grads = finish(
        grad_small, grad_qkv, w_qkv, gain_attn.reshape(1, -1), grad_tokens, shards[:3], lengths, narrow
    )
    grad_gain_attn, grad_w_down, grad_w_up, grad_w_out, *grads = grads
    grad_gain_attn, *grads = [g.reshape(-1) for g in [grad_gain_attn] + grads]
    grad_b_query, grad_b_value, grad_b_out, grad_gain_mlp, grad_b_down, grad_b_up = grads
    as_rows = lambda v: jnp.transpose(v, (1, 2, 0)).reshape(resid.shape)
    return (
        as_rows(result),
        as_rows(grad_x),
        grad_gain_attn,
        grad_w_qkv,
        grad_b_query,
        grad_b_value,
        grad_w_out,
        grad_b_out,
        grad_gain_mlp,
        grad_w_up,
        grad_b_up,
        grad_w_down,
        grad_b_down,
    )


def load_padded(ref, lane, narrow):
    return jnp.where(lane < narrow, ref[...].astype(F32), 0.0)


def norm_qkv_kernel(narrow, x_ref, gain_ref, w_ref, bias_ref, normed_ref, qkv_ref):
    rows, width = x_ref.shape
    lane = lane_index((rows, width))
    x = load_padded(x_ref, lane, narrow)
    whole = jnp.where(lane < narrow, x, -row_sum(x))
    factor = lax.rsqrt(row_sum(whole * whole) / width + epsilon)
    normed = (whole * factor * gain_ref[...]).astype(BF16)
    normed_ref[...] = normed
    for n in range(w_ref.shape[1] // width):
        cols = slice(n * width, (n + 1) * width)
        qkv_ref[:, cols] = (dot(normed, w_ref[:, cols]) + bias_ref[:, cols]).astype(BF16)


def norm_qkv(x, gain, w_qkv, bias, block=512):
    tokens, narrow = x.shape
    width = narrow + 1
    wide = w_qkv.shape[1]
    return pl.pallas_call(
        functools.partial(norm_qkv_kernel, narrow),
        grid=(tokens // block,),
        in_specs=[
            pl.BlockSpec((block, width), lambda i: (i, 0)),
            pl.BlockSpec((1, width), lambda i: (0, 0)),
            pl.BlockSpec((width, wide), lambda i: (0, 0)),
            pl.BlockSpec((1, wide), lambda i: (0, 0)),
        ],
        out_specs=[
            pl.BlockSpec((block, width), lambda i: (i, 0)),
            pl.BlockSpec((block, wide), lambda i: (i, 0)),
        ],
        out_shape=[
            jax.ShapeDtypeStruct((tokens, width), BF16),
            jax.ShapeDtypeStruct((tokens, wide), BF16),
        ],
        compiler_params=pltpu.CompilerParams(vmem_limit_bytes=vmem_grant),
        name="norm_qkv",
    )(x, gain, w_qkv, bias)


def plain_mlp_kernel(
    narrow, chunk,
    x_ref, cot_ref, att_ref, w_out_ref, w_up_ref, w_down_ref, b_out_ref, gain_ref, b_up_ref, b_down_ref,
    out_ref, act_ref, dh_ref, n2_ref, d2_ref, df_ref, dmid_ref, datt_ref, gbd_ref, gbu_ref, gg_ref, gbo_ref,
):
    rows, width = x_ref.shape
    ff = w_up_ref.shape[1]
    lane = lane_index((rows, width))
    inside = lane < narrow

    @pl.when(pl.program_id(0) == 0)
    def _():
        for ref in (gbd_ref, gbu_ref, gg_ref, gbo_ref):
            ref[...] = jnp.zeros_like(ref)

    branch = dot(att_ref[...], w_out_ref[...]) + b_out_ref[...]
    up = load_padded(cot_ref, lane, narrow)
    d2 = up - row_sum(up) / width
    gbd_ref[...] += jnp.sum(d2, axis=0, keepdims=True)
    d2 = d2.astype(BF16)
    d2_ref[...] = d2
    branch = branch - row_sum(branch) / width
    middle = jnp.where(inside, load_padded(x_ref, lane, narrow) + branch, 0.0)
    whole = jnp.where(inside, middle, -row_sum(middle))
    factor = lax.rsqrt(row_sum(whole * whole) / width + epsilon)
    scaled = whole * factor
    n2 = (scaled * gain_ref[...]).astype(BF16)
    n2_ref[...] = n2

    def stage(n):
        cols = slice(n * chunk, (n + 1) * chunk)
        return dot(n2, w_up_ref[:, cols]), dot(d2, w_down_ref[cols, :], NT)

    count = ff // chunk
    ahead = stage(0)
    for n in range(count):
        cols = slice(n * chunk, (n + 1) * chunk)
        hidden, d_act = ahead
        if n + 1 < count:
            ahead = stage(n + 1)
        hidden = hidden + b_up_ref[:, cols]
        square = hidden * hidden
        half = 0.5 + 0.5 * jnp.tanh(hidden * (gelu_c0 + gelu_c1 * square))
        active = hidden * half
        slope = half + active * (1.0 - half) * (2.0 * gelu_c0 + (6.0 * gelu_c1) * square)
        act_ref[:, cols] = active.astype(BF16)
        d_hidden = d_act * slope
        gbu_ref[:, cols] += jnp.sum(d_hidden, axis=0, keepdims=True)
        dh_ref[:, cols] = d_hidden.astype(BF16)
    dn2 = dot(dh_ref[...], w_up_ref[...], NT)
    b2 = dot(act_ref[...], w_down_ref[...]) + b_down_ref[...]
    gg_ref[...] += jnp.sum(dn2 * scaled, axis=0, keepdims=True)
    e = dn2 * gain_ref[...]
    dwhole = factor * (e - scaled * (row_sum(e * scaled) / width))
    last = row_sum(jnp.where(lane == narrow, dwhole, 0.0))
    d_mid = jnp.where(inside, up + dwhole - last, 0.0)
    dmid_ref[...] = d_mid
    d_first = d_mid - row_sum(d_mid) / width
    gbo_ref[...] += jnp.sum(d_first, axis=0, keepdims=True)
    d_first = d_first.astype(BF16)
    df_ref[...] = d_first
    datt_ref[...] = dot(d_first, w_out_ref[...], NT).astype(BF16)
    out_ref[...] = (middle + b2 - row_sum(b2) / width).astype(BF16)


def plain_mlp(x, cot, att, w_out, w_up, w_down, b_out, gain, b_up, b_down, block=256, chunk=512):
    tokens, narrow = x.shape
    width = narrow + 1
    ff = w_up.shape[1]
    per_token = lambda n: pl.BlockSpec((block, n), lambda i: (i, 0))
    fixed = lambda *shape: pl.BlockSpec(shape, lambda i: (0, 0))
    return pl.pallas_call(
        functools.partial(plain_mlp_kernel, narrow, chunk),
        grid=(tokens // block,),
        in_specs=[per_token(width)] * 3
        + [fixed(width, width), fixed(width, ff), fixed(ff, width)]
        + [fixed(1, width), fixed(1, width), fixed(1, ff), fixed(1, width)],
        out_specs=[per_token(width), per_token(ff), per_token(ff)]
        + [per_token(width)] * 5
        + [fixed(1, width), fixed(1, ff), fixed(1, width), fixed(1, width)],
        out_shape=[
            jax.ShapeDtypeStruct((tokens, narrow), BF16),
            jax.ShapeDtypeStruct((tokens, ff), BF16),
            jax.ShapeDtypeStruct((tokens, ff), BF16),
            jax.ShapeDtypeStruct((tokens, width), BF16),
            jax.ShapeDtypeStruct((tokens, width), BF16),
            jax.ShapeDtypeStruct((tokens, width), BF16),
            jax.ShapeDtypeStruct((tokens, width), F32),
            jax.ShapeDtypeStruct((tokens, width), BF16),
            jax.ShapeDtypeStruct((1, width), F32),
            jax.ShapeDtypeStruct((1, ff), F32),
            jax.ShapeDtypeStruct((1, width), F32),
            jax.ShapeDtypeStruct((1, width), F32),
        ],
        compiler_params=pltpu.CompilerParams(vmem_limit_bytes=vmem_grant),
        name="mlp",
    )(x, cot, att, w_out, w_up, w_down, b_out, gain, b_up, b_down)


def wgrad_kernel(left_ref, right_ref, out_ref):
    out_ref[...] = dot(left_ref[...], right_ref[...], TN).astype(out_ref.dtype)


def wgrad(left, right, rows, cols):
    tokens, m = left.shape
    n = right.shape[1]
    return pl.pallas_call(
        wgrad_kernel,
        grid=(m // rows, n // cols),
        in_specs=[
            pl.BlockSpec((tokens, rows), lambda i, j: (0, i)),
            pl.BlockSpec((tokens, cols), lambda i, j: (0, j)),
        ],
        out_specs=pl.BlockSpec((rows, cols), lambda i, j: (i, j)),
        out_shape=jax.ShapeDtypeStruct((m, n), BF16),
        compiler_params=pltpu.CompilerParams(vmem_limit_bytes=vmem_grant),
        name="wgrad",
    )(left, right)


def plain_back_kernel(
    narrow, x_ref, dq_ref, dk_ref, dv_ref, w_ref, gain_ref, dmid_ref, out_ref, gg_ref
):
    rows, width = x_ref.shape
    lane = lane_index((rows, width))
    inside = lane < narrow

    @pl.when(pl.program_id(0) == 0)
    def _():
        gg_ref[...] = jnp.zeros_like(gg_ref)

    dn = dot(dq_ref[...], w_ref[:, 0:width], NT)
    dn = dn + dot(dk_ref[...], w_ref[:, width : 2 * width], NT)
    dn = dn + dot(dv_ref[...], w_ref[:, 2 * width : 3 * width], NT)
    x = load_padded(x_ref, lane, narrow)
    whole = jnp.where(inside, x, -row_sum(x))
    factor = lax.rsqrt(row_sum(whole * whole) / width + epsilon)
    scaled = whole * factor
    gg_ref[...] += jnp.sum(dn * scaled, axis=0, keepdims=True)
    e = dn * gain_ref[...]
    dwhole = factor * (e - scaled * (row_sum(e * scaled) / width))
    last = row_sum(jnp.where(lane == narrow, dwhole, 0.0))
    out_ref[...] = (dmid_ref[...] + dwhole - last).astype(BF16)


def plain_back(x, dq, dk, dv, w_qkv, gain, dmid, block=512):
    tokens, narrow = x.shape
    width = narrow + 1
    per_token = lambda n: pl.BlockSpec((block, n), lambda i: (i, 0))
    fixed = lambda *shape: pl.BlockSpec(shape, lambda i: (0, 0))
    return pl.pallas_call(
        functools.partial(plain_back_kernel, narrow),
        grid=(tokens // block,),
        in_specs=[per_token(width)] * 4
        + [fixed(width, 3 * width), fixed(1, width), per_token(width)],
        out_specs=[per_token(width), fixed(1, width)],
        out_shape=[
            jax.ShapeDtypeStruct((tokens, narrow), BF16),
            jax.ShapeDtypeStruct((1, width), F32),
        ],
        compiler_params=pltpu.CompilerParams(vmem_limit_bytes=vmem_grant),
        name="back",
    )(x, dq, dk, dv, w_qkv, gain, dmid)


def fwd_kernel(docs, hd, blk, back, q_ref,k_ref,v_ref,segc_ref,segr_ref,o_ref,lse_ref,bias_ref,qx_ref,kx_ref):
    seq=q_ref.shape[0]; lanes=2*hd
    nb=seq//blk
    pair=pl.program_id(1)
    lane=lax.broadcasted_iota(jnp.int32,(seq,lanes),1)
    @pl.when(pair==0)
    def _():
        segc=segc_ref[...]
        for i in range(nb):
            sq=segc[i*blk:(i+1)*blk]; sk=segr_ref[:,i*blk:(i+1)*blk]
            r=lax.broadcasted_iota(jnp.int32,(blk,blk),0); c=lax.broadcasted_iota(jnp.int32,(blk,blk),1)
            bias_ref[i]=jnp.where((c<=r)&(sq==sk),0.0,masked_score)
        for h in range(2):
            sub=lane-(1-h)*hd
            seg=jnp.broadcast_to(jnp.minimum(segc,docs),(seq,lanes))
            in_aug=(sub>=0)&(sub<=docs)
            hot=seg==sub
            qx_ref[h]=jnp.where(in_aug&~hot,masked_score,0.0).astype(BF16)
            kx_ref[h]=jnp.where(in_aug&hot,1.0,0.0).astype(BF16)
    scale=hd**-0.5
    q=q_ref[...]*jnp.asarray(scale,BF16); k=k_ref[...]; v=v_ref[...]
    own=[lane<hd, lane>=hd]
    qa=[jnp.where(own[h],q,qx_ref[h]) for h in range(2)]
    ka=[jnp.where(own[h],k,kx_ref[h]) for h in range(2)]
    va=[jnp.where(own[h],v,jnp.asarray(1.0,BF16)) for h in range(2)]
    units=[(i,h) for i in range(nb) for h in range(2)]
    kt=[a.T for a in ka]
    def score(u):
        i,h=u
        lo=max(0,i-back)*blk; hi=(i+1)*blk; d0=i*blk
        qb=qa[h][d0:hi]
        parts=[]
        if lo<d0: parts.append(dot(qb,kt[h][:,lo:d0]))
        parts.append(dot(qb,kt[h][:,d0:hi])+bias_ref[i])
        return parts
    nxt=score(units[0])
    keep={}
    for n,(i,h) in enumerate(units):
        lo=max(0,i-back)*blk; hi=(i+1)*blk; d0=i*blk
        parts=nxt
        if n+1<len(units): nxt=score(units[n+1])
        m=functools.reduce(jnp.maximum,[jnp.max(p,axis=1,keepdims=True) for p in parts])
        ps=[jnp.exp(p-m).astype(BF16) for p in parts]
        o=dot(ps[-1],va[h][d0:hi])
        if lo<d0: o=o+dot(ps[0],va[h][lo:d0])
        l=pltpu.roll(o,hd,1)
        keep[h]=(o/l,m+jnp.log(l))
        if h==1:
            ln=lane[:blk]
            o_ref[d0:hi,:]=jnp.where(ln<hd,keep[0][0],keep[1][0]).astype(BF16)
            lse_ref[d0:hi,:]=jnp.where(ln<hd,keep[0][1],keep[1][1])


def attn_fwd(qkv,segments,docs,heads,blk=256,most=512):
    rows,seq=segments.shape; T,w=qkv.shape
    d=w//3; hd=d//heads; lanes=2*hd; pairs=heads//2
    back=-(-(most-1)//blk)
    spec=lambda off: pl.BlockSpec((seq,lanes),lambda r,p:(r,off+p))
    return pl.pallas_call(
        functools.partial(fwd_kernel,docs,hd,blk,back),
        grid=(rows,pairs),
        in_specs=[spec(0),spec(pairs),spec(2*pairs),
                  pl.BlockSpec((None,seq,1),lambda r,p:(r,0,0)),pl.BlockSpec((None,1,seq),lambda r,p:(r,0,0))],
        out_specs=[spec(0),spec(0)],
        out_shape=[jax.ShapeDtypeStruct((T,d),BF16),jax.ShapeDtypeStruct((T,d),F32)],
        scratch_shapes=[pltpu.VMEM((seq//blk,blk,blk),F32),pltpu.VMEM((2,seq,lanes),BF16),pltpu.VMEM((2,seq,lanes),BF16)],
        compiler_params=pltpu.CompilerParams(vmem_limit_bytes=vmem_grant),
    )(qkv,qkv,qkv,segments[:,:,None],segments[:,None,:])

def bwd_kernel(docs, hd, blk, back, q_ref,k_ref,v_ref,o_ref,do_ref,lse_ref,segc_ref,segr_ref,
               dq_ref,dk_ref,dv_ref,sq_ref,sv_ref,bias_ref,qx_ref,kx_ref,dqa_ref):
    seq=q_ref.shape[0]; lanes=2*hd
    nb=seq//blk
    pair=pl.program_id(1)
    lane=lax.broadcasted_iota(jnp.int32,(seq,lanes),1)
    @pl.when(pair==0)
    def _():
        segc=segc_ref[...]
        for i in range(nb):
            sk=segc[i*blk:(i+1)*blk]; sq=segr_ref[:,i*blk:(i+1)*blk]
            r=lax.broadcasted_iota(jnp.int32,(blk,blk),0); c=lax.broadcasted_iota(jnp.int32,(blk,blk),1)
            bias_ref[i]=jnp.where((r<=c)&(sq==sk),0.0,masked_score)
        for h in range(2):
            sub=lane-(1-h)*hd
            seg=jnp.broadcast_to(jnp.minimum(segc,docs),(seq,lanes))
            in_aug=(sub>=0)&(sub<=docs)
            hot=seg==sub
            qx_ref[h]=jnp.where(in_aug&~hot,masked_score,0.0).astype(BF16)
            kx_ref[h]=jnp.where((in_aug&hot)|((sub>docs)&(sub<=docs+3)),1.0,0.0).astype(BF16)
    scale=hd**-0.5
    q=q_ref[...]*jnp.asarray(scale,BF16); k=k_ref[...]; v=v_ref[...]; do=do_ref[...]
    prod=do.astype(F32)*o_ref[...].astype(F32)
    hi_=prod.astype(BF16); lo_=(prod-hi_.astype(F32)).astype(BF16)
    r=lax.broadcasted_iota(jnp.int32,(lanes,lanes),0); c=lax.broadcasted_iota(jnp.int32,(lanes,lanes),1)
    ones=jnp.where((r<hd)!=(c<hd),1.0,0.0).astype(BF16)
    delta=-(dot(hi_,ones)+dot(lo_,ones))
    nl=-pltpu.roll(lse_ref[...],hd,1)
    d3=split3(delta); l3=split3(nl)
    own=[lane<hd, lane>=hd]
    qa=[];ka=[];va=[];da=[]
    one=jnp.asarray(1.0,BF16); zero=jnp.asarray(0.0,BF16)
    for h in range(2):
        sub=lane-(1-h)*hd
        qx=qx_ref[h]
        vx=jnp.where((sub>=0)&(sub<3),1.0,0.0).astype(BF16)
        dx=jnp.zeros_like(do)
        for n in range(3):
            qx=jnp.where(sub==docs+1+n,l3[n],qx)
            dx=jnp.where(sub==n,d3[n],dx)
        qa.append(jnp.where(own[h],q,qx))
        ka.append(jnp.where(own[h],k,kx_ref[h]))
        va.append(jnp.where(own[h],v,vx))
        da.append(jnp.where(own[h],do,dx))
    for h in range(2):
        dqa_ref[h]=jnp.zeros((seq,lanes),F32)
    ln=lane[:blk]
    sv=jnp.zeros((1,lanes),F32)
    units=[]
    for j in range(nb):
        d0=j*blk; hi=(j+1)*blk; top=min(nb,j+1+back)*blk
        for h in range(2):
            units.append((j,h,d0,hi,top))
    def stage(u):
        j,h,d0,hi,top=u
        st=dot(ka[h][d0:hi],qa[h][d0:top],NT)
        dpt=dot(va[h][d0:hi],da[h][d0:top],NT)
        return st,dpt
    look=1
    queue=[stage(u) for u in units[:look]]
    for n,(j,h,d0,hi,top) in enumerate(units):
        st,dpt=queue.pop(0)
        if n+look<len(units): queue.append(stage(units[n+look]))
        st0=st[:,:blk]+bias_ref[j]
        st=jnp.concatenate([st0,st[:,blk:]],axis=1) if top>hi else st0
        pt=jnp.exp(st)
        dst=(pt*dpt).astype(BF16)
        pt=pt.astype(BF16)
        dv=dot(pt,do[d0:top]); dk=dot(dst,q[d0:top])
        dqa_ref[h,d0:top,:]+=dot(dst,k[d0:hi],TN)
        if h==0:
            first=(dv,dk)
        else:
            dvf=jnp.where(ln<hd,first[0],dv)
            sv=sv+jnp.sum(dvf,axis=0,keepdims=True)
            dv_ref[d0:hi,:]=dvf.astype(BF16)
            dk_ref[d0:hi,:]=jnp.where(ln<hd,first[1],dk).astype(BF16)
    dq=jnp.where(lane<hd,dqa_ref[0],dqa_ref[1])*scale
    dq_ref[...]=dq.astype(BF16)
    sq_ref[...]=jnp.sum(dq,axis=0,keepdims=True)
    sv_ref[...]=sv

def attn_bwd(qkv,att,datt,lse,segments,docs,heads,blk=256,most=512):
    rows,seq=segments.shape; T,w=qkv.shape
    d=w//3; hd=d//heads; lanes=2*hd; pairs=heads//2
    back=-(-(most-1)//blk)
    spec=lambda off: pl.BlockSpec((seq,lanes),lambda r,p:(r,off+p))
    vec=pl.BlockSpec((None,1,lanes),lambda r,p:(r,0,p))
    return pl.pallas_call(
        functools.partial(bwd_kernel,docs,hd,blk,back),
        grid=(rows,pairs),
        in_specs=[spec(0),spec(pairs),spec(2*pairs),spec(0),spec(0),spec(0),
                  pl.BlockSpec((None,seq,1),lambda r,p:(r,0,0)),pl.BlockSpec((None,1,seq),lambda r,p:(r,0,0))],
        out_specs=[spec(0),spec(0),spec(0),vec,vec],
        out_shape=[jax.ShapeDtypeStruct((T,d),BF16)]*3+[jax.ShapeDtypeStruct((rows,1,d),F32)]*2,
        scratch_shapes=[pltpu.VMEM((seq//blk,blk,blk),F32),pltpu.VMEM((2,seq,lanes),BF16),pltpu.VMEM((2,seq,lanes),BF16),pltpu.VMEM((2,seq,lanes),F32)],
        compiler_params=pltpu.CompilerParams(vmem_limit_bytes=vmem_grant),
    )(qkv,qkv,qkv,att,datt,lse,segments[:,:,None],segments[:,None,:])


def segment_ids(doc_lengths, pad_count, seq_len):
    docs = doc_lengths.shape[-1]
    upto = jnp.arange(docs)[None, :] <= jnp.arange(docs)[:, None]
    doc_ends = jnp.sum(jnp.where(upto[None], doc_lengths[:, None, :], 0), axis=-1)
    positions = jnp.arange(seq_len, dtype=jnp.int32)
    counted = jnp.sum((doc_ends[:, :, None] <= positions[None, None, :]).astype(jnp.int32), axis=1)
    padding = positions[None, :] >= seq_len - pad_count[:, None]
    return jnp.where(padding, docs + positions[None, :], counted)


def as_row(vector):
    return vector.astype(F32)[None]


def plain_body(
    resid, lengths, pad_len, gain_attn, w_qkv, b_query, b_value, w_out, b_out, gain_mlp, w_up, b_up, w_down, b_down,
    cotangent,
):
    narrow = resid.shape[3]
    width = narrow + 1
    seq = resid.shape[2]
    docs = lengths.shape[2]
    segments = segment_ids(lengths.reshape(-1, docs), pad_len.reshape(-1), seq)
    x = resid.reshape(-1, narrow)
    cot = cotangent.reshape(-1, narrow)
    every = lambda v: lax.all_gather(v, AX, axis=0, tiled=True)
    vectors = [every(v) for v in (gain_attn, b_query, b_value, b_out, gain_mlp, b_down, b_up)]
    matrices = [every(v) for v in (w_qkv, w_out, w_up, w_down)]
    gain_attn, b_query, b_value, b_out, gain_mlp, b_down, b_up = [as_row(v) for v in vectors]
    w_qkv, w_out, w_up, w_down = matrices
    qkv_bias = jnp.concatenate([b_query, jnp.zeros_like(b_query), b_value], axis=1)
    normed_first, qkv = norm_qkv(x, gain_attn, w_qkv, qkv_bias)
    attended, log_sums = attn_fwd(qkv, segments, docs, HEADS, most=MOST)
    (
        result, active, d_hidden, normed_second, d_second, d_first, d_middle, d_attended,
        grad_b_down, grad_b_up, grad_gain_mlp, grad_b_out,
    ) = plain_mlp(x, cot, attended, w_out, w_up, w_down, b_out, gain_mlp, b_up, b_down)
    ff = w_up.shape[1]
    grad_w_down = wgrad(active, d_second, 512, width)
    grad_w_up = wgrad(normed_second, d_hidden, width, 512)
    grad_w_out = wgrad(attended, d_first, width, width)
    d_query, d_keys, d_values, sum_query, sum_value = attn_bwd(
        qkv, attended, d_attended, log_sums, segments, docs, HEADS, most=MOST
    )
    grads_qkv = [wgrad(normed_first, d, width, width) for d in (d_query, d_keys, d_values)]
    grad_input, grad_gain_attn = plain_back(x, d_query, d_keys, d_values, w_qkv, gain_attn, d_middle)
    vectors = [
        grad_gain_attn[0],
        jnp.sum(sum_query, axis=(0, 1)),
        jnp.sum(sum_value, axis=(0, 1)),
        grad_b_out[0],
        grad_gain_mlp[0],
        grad_b_down[0],
        grad_b_up[0],
    ]
    own = lambda v: lax.psum_scatter(v.astype(F32), AX, scatter_dimension=0, tiled=True)
    vectors = [own(v) for v in vectors]
    matrices = [own(v) for v in [grad_w_down, grad_w_up, grad_w_out] + grads_qkv]
    grad_gain_attn, grad_b_query, grad_b_value, grad_b_out, grad_gain_mlp, grad_b_down, grad_b_up = vectors
    grad_w_down, grad_w_up, grad_w_out = matrices[:3]
    grad_w_qkv = jnp.concatenate(matrices[3:], axis=1)
    return (
        result.reshape(resid.shape),
        grad_input.reshape(resid.shape),
        grad_gain_attn,
        grad_w_qkv,
        grad_b_query,
        grad_b_value,
        grad_w_out,
        grad_b_out,
        grad_gain_mlp,
        grad_w_up,
        grad_b_up,
        grad_w_down,
        grad_b_down,
    )


def slice_sizes(mesh, rows):
    wide, narrow = mesh.shape["wide"], mesh.shape["narrow"]
    depth = len({getattr(d, "coords", (0, 0, 0))[1] for d in mesh.devices.flat})
    per = rows // (wide * narrow)
    if per % 8 or 4 * per > 128 or rows % (wide * narrow) or narrow % 2 or depth != narrow // 2 or wide % depth:
        return None
    return (wide // depth, depth, narrow // 2)


def solution(mesh):
    row_split = P(None, AX)
    own = P(AX)

    def program(*args):
        sizes = slice_sizes(mesh, args[3].shape[0])
        return jax.shard_map(
            plain_body if sizes is None else functools.partial(body, sizes),
            mesh=mesh,
            in_specs=(row_split,) * 3 + (own,) * 11 + (row_split,),
            out_specs=(row_split,) * 2 + (own,) * 11,
            check_vma=False,
        )(*args)

    return program
```

```python
import functools
import math
import jax
import jax.numpy as jnp
from jax import lax
from jax.experimental import pallas as pl
from jax.experimental.pallas import tpu as pltpu
from jax.sharding import PartitionSpec as P

F32 = jnp.float32
BF16 = jnp.bfloat16
epsilon = 1e-05
vmem_grant = 60 << 20
NT = (((1,), (1,)), ((), ()))
TN = (((0,), (0,)), ((), ()))
NN = (((1,), (0,)), ((), ()))
gelu_c0 = math.sqrt(2.0 / math.pi)
gelu_c1 = gelu_c0 * 0.044715


def dot(left, right, dims=NN):
    return lax.dot_general(left, right, dims, preferred_element_type=F32)


def lane_index(shape):
    return lax.broadcasted_iota(jnp.int32, shape, 1)


def row_sum(values):
    return jnp.sum(values, axis=1, keepdims=True)


AX = ("wide", "narrow")
HEADS = 12
MOST = 512
masked_score = -1e30


MESH = pl.DeviceIdType.MESH


class Place:
    def __init__(self, nz, ny, nx):
        self.nz, self.ny, self.nx = nz, ny, nx
        wide = lax.axis_index("wide")
        narrow = lax.axis_index("narrow")
        self.z, self.y = wide // ny, wide % ny
        self.x, self.c = narrow // 2, narrow % 2

    def block(self, third, second, deep):
        along_y = jnp.where(self.c == 0, second, third)
        along_x = jnp.where(self.c == 0, third, second)
        return (self.z + deep) % self.nz, (self.y + along_y) % self.ny, (self.x + along_x) % self.nx

    def device(self, third, second, deep, other_core=False):
        z, y, x = self.block(third, second, deep)
        core = 1 - self.c if other_core else self.c
        return (z * self.ny + y, x * 2 + core)

    def greet(self):
        barrier = pltpu.get_barrier_semaphore()
        partners = [self.device(0, 0, k) for k in range(1, self.nz)]
        partners += [self.device(0, k, 0) for k in range(1, self.nx)]
        partners += [self.device(k, 0, 0) for k in range(1, self.nx)]
        partners.append(self.device(0, 0, 0, True))
        for partner in partners:
            pl.semaphore_signal(barrier, inc=1, device_id=partner, device_id_type=MESH)
        pl.semaphore_wait(barrier, len(partners))


class Transfer:
    def __init__(self, place, send, recv):
        self.place, self.send, self.recv = place, send, recv
        self.index = {key: n for n, key in enumerate(self.keys(place.nz, place.nx))}

    def copy(self, key):
        source, target, device = self.ends(key)
        n = self.index[key]
        return pltpu.make_async_remote_copy(
            src_ref=source,
            dst_ref=target,
            send_sem=self.send.at[n],
            recv_sem=self.recv.at[n],
            device_id=device,
            device_id_type=MESH,
        )

    def start(self, *key):
        self.copy(key).start()

    def arrived(self, *key):
        self.copy(key).wait_recv()

    def sent(self):
        for key in self.index:
            self.copy(key).wait_send()


class Gather(Transfer):
    def __init__(self, place, shard, full, send, recv, local):
        super().__init__(place, send, recv)
        self.shard, self.full, self.local = shard, full, local

    @staticmethod
    def keys(nz, n2):
        out = [("z", k) for k in range(1, nz)]
        out += [("s", k, d) for k in range(1, n2) for d in range(nz)]
        out += [("t", k, b, d) for k in range(1, n2) for b in range(n2) for d in range(nz)]
        out += [("c", a, b, d) for a in range(n2) for b in range(n2) for d in range(nz)]
        return out

    def ends(self, key):
        p = self.place
        kind = key[0]
        if kind == "z":
            offset, device = (0, 0, 0), p.device(0, 0, key[1])
        elif kind == "s":
            offset, device = (0, 0, key[2]), p.device(0, key[1], 0)
        elif kind == "t":
            offset, device = (0, key[2], key[3]), p.device(key[1], 0, 0)
        else:
            offset, device = key[1:], p.device(0, 0, 0, True)
        z, y, x = p.block(*offset)
        target = self.full.at[z, y, x, p.c]
        return (self.shard if offset == (0, 0, 0) else target), target, device

    def own(self):
        p = self.place
        return pltpu.make_async_copy(self.shard, self.full.at[p.z, p.y, p.x, p.c], self.local)

    def spread(self, a, b, d):
        if a == 0:
            if b == 0:
                for k in range(1, self.place.nx):
                    self.start("s", k, d)
            for k in range(1, self.place.nx):
                self.start("t", k, b, d)
        self.start("c", a, b, d)

    def begin(self):
        for k in range(1, self.place.nz):
            self.start("z", k)
        self.spread(0, 0, 0)
        self.own().start()

    def steps(self):
        nz, n2 = self.place.nz, self.place.nx

        def step(key, a, b, d):
            def run():
                self.arrived(*key)
                self.spread(a, b, d)

            return run

        out = [step(("z", k), 0, 0, nz - k) for k in range(1, nz)]
        order = [0] + [nz - k for k in range(1, nz)]
        out += [step(("s", k, d), 0, n2 - k, d) for d in order for k in range(1, n2)]
        out += [
            step(("t", k, b, d), n2 - k, b, d) for b in range(n2) for d in order for k in range(1, n2)
        ]
        return out

    def landed(self):
        for key in self.index:
            if key[0] == "c":
                self.arrived(*key)
        self.own().wait()


class Scatter(Transfer):
    def __init__(self, place, terms, out, buffers, send, recv, load):
        super().__init__(place, send, recv)
        self.terms, self.out = terms, out
        self.mine, self.r0, self.r1, self.r2, self.r3 = buffers
        self.load = load

    @staticmethod
    def keys(nz, n2):
        out = [("c", a, b, d) for a in range(n2) for b in range(n2) for d in range(nz)]
        out += [("t", a, b, d) for a in range(1, n2) for b in range(n2) for d in range(nz)]
        out += [("s", b, d) for b in range(1, n2) for d in range(nz)]
        out += [("z", d) for d in range(1, nz)]
        return out

    @staticmethod
    def buffers(nz, n2, block, dtype):
        counts = (nz * n2 * n2, nz * n2 * n2, nz * n2 * (n2 - 1), nz * (n2 - 1), nz - 1)
        return [pltpu.VMEM((n,) + block, dtype) for n in counts]

    def slot(self, a, b, d):
        return (a * self.place.nx + b) * self.place.nz + d

    def order(self):
        near = list(range(1, self.place.nx)) + [0]
        deep = list(range(1, self.place.nz)) + [0]
        return [(a, b, d) for a in near for b in near for d in deep]

    def ends(self, key):
        p = self.place
        kind = key[0]
        if kind == "c":
            a, b, d = key[1:]
            z, y, x = p.block(a, b, d)
            return self.terms.at[z, y, x, 1 - p.c], self.r0.at[self.slot(b, a, d)], p.device(0, 0, 0, True)
        if kind == "t":
            a, b, d = key[1:]
            return self.mine.at[self.slot(a, b, d)], self.r1.at[self.slot(a - 1, b, d)], p.device(a, 0, 0)
        if kind == "s":
            b, d = key[1:]
            return self.mine.at[self.slot(0, b, d)], self.r2.at[self.slot(0, b - 1, d)], p.device(0, b, 0)
        d = key[1]
        return self.mine.at[self.slot(0, 0, d)], self.r3.at[d - 1], p.device(0, 0, d)

    def loading(self, a, b, d):
        p = self.place
        z, y, x = p.block(a, b, d)
        n = self.slot(a, b, d)
        return pltpu.make_async_copy(self.terms.at[z, y, x, p.c], self.mine.at[n], self.load.at[n])

    def begin(self):
        for a, b, d in self.order():
            self.start("c", b, a, d)
            self.loading(a, b, d).start()

    def gathered(self, a, b, d):
        p = self.place
        self.loading(a, b, d).wait()
        self.arrived("c", b, a, d)
        n = self.slot(a, b, d)
        parts = [self.mine.at[n], self.r0.at[n]]
        if a == 0:
            for k in range(1, p.nx):
                self.arrived("t", k, b, d)
                parts.append(self.r1.at[self.slot(k - 1, b, d)])
            if b == 0:
                for k in range(1, p.nx):
                    self.arrived("s", k, d)
                    parts.append(self.r2.at[self.slot(0, k - 1, d)])
        return parts

    def add(self, target, parts):
        def step(slab, _):
            total = parts[0][slab].astype(F32)
            for part in parts[1:]:
                total = total + part[slab].astype(F32)
            target[slab] = total.astype(target.dtype)
            return 0

        lax.fori_loop(0, target.shape[0], step, 0)

    def steps(self):
        def step(a, b, d):
            def run():
                parts = self.gathered(a, b, d)
                if (a, b, d) == (0, 0, 0):
                    for k in range(1, self.place.nz):
                        self.arrived("z", k)
                        parts.append(self.r3.at[k - 1])
                    self.add(self.out, parts)
                    return
                self.add(parts[0], parts)
                if a:
                    self.start("t", a, b, d)
                elif b:
                    self.start("s", b, d)
                else:
                    self.start("z", d)

            return run

        return [step(a, b, d) for a, b, d in self.order()]


def semaphores(count, keys, locals_):
    return [
        pltpu.SemaphoreType.DMA((count, keys)),
        pltpu.SemaphoreType.DMA((count, keys)),
        pltpu.SemaphoreType.DMA((count, locals_)),
    ]


def split3(value):
    first = value.astype(BF16)
    rest = value - first.astype(F32)
    second = rest.astype(BF16)
    return first, second, (rest - second.astype(F32)).astype(BF16)


def to_rows(x_ref, m, cols, narrow):
    value = x_ref[:, m, cols].astype(F32).T
    return jnp.where(lane_index(value.shape) < narrow, value, 0.0)


def from_rows(out_ref, m, cols, value):
    out_ref[:, m, cols] = value.T.astype(out_ref.dtype)


def segment_of(lengths_ref, pad_ref, row, positions, seq):
    docs = lengths_ref.shape[1]
    end = 0
    counted = jnp.zeros_like(positions)
    for doc in range(docs):
        end = end + lengths_ref[row, doc]
        counted = counted + (end <= positions).astype(jnp.int32)
    return jnp.where(positions >= seq - pad_ref[0, row], docs + positions, counted)


def attention_masks(lengths_ref, pad_ref, row, bias_ref, qx_ref, kx_ref, block, transposed):
    docs = lengths_ref.shape[1]
    _, seq, lanes = qx_ref.shape
    head = lanes // 2
    down = segment_of(lengths_ref, pad_ref, row, lax.broadcasted_iota(jnp.int32, (seq, lanes), 0), seq)
    across = segment_of(lengths_ref, pad_ref, row, lax.broadcasted_iota(jnp.int32, (1, seq), 1), seq)
    r = lax.broadcasted_iota(jnp.int32, (block, block), 0)
    c = lax.broadcasted_iota(jnp.int32, (block, block), 1)
    causal = r <= c if transposed else c <= r
    for i in range(seq // block):
        part = slice(i * block, (i + 1) * block)
        same = jnp.concatenate([down[part]] * (block // lanes), axis=1) == across[:, part]
        bias_ref[i] = jnp.where(causal & same, 0.0, masked_score)
    lane = lane_index((seq, lanes))
    hot_at = jnp.minimum(down, docs)
    for h in range(2):
        spare = lane - (1 - h) * head
        used = (spare >= 0) & (spare <= docs)
        hot = hot_at == spare
        qx_ref[h] = jnp.where(used & ~hot, masked_score, 0.0).astype(BF16)
        ones = (spare > docs) & (spare <= docs + 3)
        kx_ref[h] = jnp.where((used & hot) | ones, 1.0, 0.0).astype(BF16)


def attention_forward(q, k, v, bias_ref, qx_ref, kx_ref, block, back, att_ref, lse_ref):
    seq, lanes = q.shape
    head = lanes // 2
    lane = lane_index((seq, lanes))
    q = q * jnp.asarray(head**-0.5, BF16)
    own = [lane < head, lane >= head]
    queries = [jnp.where(own[h], q, qx_ref[h]) for h in range(2)]
    keys = [jnp.where(own[h], k, kx_ref[h]) for h in range(2)]
    values = [jnp.where(own[h], v, jnp.asarray(1.0, BF16)) for h in range(2)]
    units = []
    for i in range(seq // block):
        for h in range(2):
            units.append((i, h, max(0, i - back) * block, i * block, (i + 1) * block))

    def scores(unit):
        i, h, low, start, stop = unit
        part = queries[h][start:stop]
        out = []
        if low < start:
            out.append(dot(part, keys[h][low:start], NT))
        out.append(dot(part, keys[h][start:stop], NT) + bias_ref[i])
        return out

    ahead = scores(units[0])
    for n, (i, h, low, start, stop) in enumerate(units):
        parts = ahead
        if n + 1 < len(units):
            ahead = scores(units[n + 1])
        top = functools.reduce(jnp.maximum, [jnp.max(p, axis=1, keepdims=True) for p in parts])
        probs = [jnp.exp(p - top).astype(BF16) for p in parts]
        out = dot(probs[-1], values[h][start:stop])
        if low < start:
            out = out + dot(probs[0], values[h][low:start])
        total = pltpu.roll(out, head, 1)
        result = (out / total, top + jnp.log(total))
        if h == 0:
            first = result
        else:
            left = lane[:block] < head
            att_ref[start:stop, :] = jnp.where(left, first[0], result[0]).astype(BF16)
            lse_ref[start:stop, :] = jnp.where(left, first[1], result[1])


def spread_vectors(packed, per, width):
    lanes = packed.shape[1]
    column = lane_index((lanes, width))
    owner = ((column.astype(F32) + 0.5) * (1.0 / per)).astype(jnp.int32)
    place = column - owner * per
    hot = jnp.where(place == lax.broadcasted_iota(jnp.int32, (lanes, width), 0), 1.0, 0.0).astype(BF16)
    spread = dot(packed, hot).reshape(-1, 8, width)
    shape = spread.shape
    column = lax.broadcasted_iota(jnp.int32, shape, 2)
    owner = ((column.astype(F32) + 0.5) * (1.0 / per)).astype(jnp.int32)
    return jnp.sum(jnp.where(owner == lax.broadcasted_iota(jnp.int32, shape, 0), spread, 0.0), axis=0)


FORWARD_TIMES = (
    ((1, 2, 2), (4, 4, 5, 5), (9, 9, 10, 10, 11, 11, 12, 12)),
    ((3, 4, 5), (7, 7, 8, 8), (12, 12, 13, 13, 14, 14, 15, 15)),
    ((6, 7, 8), (10, 11, 12, 13), (16, 16, 16, 16, 16, 16, 16, 16)),
)


def forward_times(plans, count):
    out = []
    for n, plan in enumerate(plans):
        nz, n2 = plan.place.nz, plan.place.nx
        items = plan.steps()
        start = 0
        for times, length in zip(FORWARD_TIMES[n], (nz - 1, nz * (n2 - 1), nz * n2 * (n2 - 1))):
            for m in range(length):
                at = times[m * len(times) // length]
                out.append((max(1, at * count // 16), items[start + m]))
            start += length
    out.sort(key=lambda entry: entry[0])
    return out


def tile_vectors(flat, per):
    length = flat.shape[1]
    vector_of = lambda f: jnp.minimum(((f.astype(F32) + 0.5) * (1.0 / per)).astype(jnp.int32), 6)
    f = lane_index((8, length))
    rows = jnp.where(vector_of(f) == lax.broadcasted_iota(jnp.int32, f.shape, 0), flat.astype(F32), 0.0)
    f = lax.broadcasted_iota(jnp.int32, (length, 128), 0)
    hot = jnp.where(f - vector_of(f) * per == lane_index(f.shape), 1.0, 0.0)
    return dot(rows.astype(BF16), hot.astype(BF16)).astype(BF16)


def forward_kernel(
    sizes, narrow, block, back, first_steps, per_ff,
    lengths_ref, pad_ref, x_ref, small_ref, wqkv_ref, wout_ref, wup_ref, wdown_ref,
    small_all, wqkv_all, wout_all, wup_all, wdown_all, vec_ref, bup_ref, normed_ref, qkv_ref, att_ref, lse_ref,
    send, recv, local, tile_s, small_s, wide_s, w_s, scaled_s, qkv_s, bias_s, qx_s, kx_s, load,
):
    step = pl.program_id(0)
    rows, seq, width = scaled_s.shape
    pairs = qkv_s.shape[0] // 3
    chunk = seq // first_steps
    place = Place(*sizes)
    ends = [
        (tile_s, small_all),
        (wqkv_ref, wqkv_all),
        (wout_ref, wout_all),
        (wup_ref, wup_all),
        (wdown_ref, wdown_all),
    ]
    plans = [Gather(place, s, f, send.at[n], recv.at[n], local.at[n, 0]) for n, (s, f) in enumerate(ends)]
    last = pl.num_programs(0) - 1
    count = first_steps + rows * pairs
    later = forward_times(plans[2:], count)

    @pl.when(step == 0)
    def _():
        place.greet()
        tile_s[0] = tile_vectors(small_ref[...], width // (small_all.shape[0] * small_all.shape[1] * small_all.shape[2] * 2))
        for plan in plans:
            plan.begin()
        for i in range(first_steps):
            for m in range(rows):
                cols = slice(i * chunk, (i + 1) * chunk)
                x = to_rows(x_ref, m, cols, narrow)
                whole = jnp.where(lane_index(x.shape) < narrow, x, -row_sum(x))
                scaled_s[m, cols, :] = whole * lax.rsqrt(row_sum(whole * whole) / width + epsilon)
        for one, two in zip(plans[0].steps(), plans[1].steps()):
            one()
            two()
        plans[0].landed()
        copy = pltpu.make_async_copy(small_all, small_s, load)
        copy.start()
        copy.wait()
        packed = small_s[...].astype(F32).reshape(-1, small_s.shape[-1]).astype(BF16)
        devices = packed.shape[0] // 8
        vec_ref[...] = spread_vectors(packed, width // devices, width)
        bup_ref[...] = spread_vectors(packed, per_ff, bup_ref.shape[1])
        plans[1].landed()
        copy = pltpu.make_async_copy(wqkv_all, wide_s, load)
        copy.start()
        copy.wait()
        for n in range(w_s.shape[1] // width):
            cols = slice(n * width, (n + 1) * width)
            w_s[:, cols] = wide_s[..., cols].astype(F32).reshape(-1, width).astype(BF16)

    for n in range(1, count):
        some = [item for at, item in later if at == n]
        if some:

            @pl.when(step == n)
            def _():
                for item in some:
                    item()

    @pl.when(step < first_steps)
    def _():
        cols = pl.ds(pl.multiple_of(step * chunk, chunk), chunk)
        normed = (scaled_s[:, cols, :].reshape(-1, width) * vec_ref[0:1, :]).astype(BF16)
        normed_ref[...] = normed.reshape(normed_ref.shape)
        for n in range(3):
            res = dot(normed, w_s[:, n * width : (n + 1) * width])
            if n != 1:
                res = res + vec_ref[1 + n // 2 : 2 + n // 2, :]
            res = res.astype(BF16)
            lanes = width // pairs
            for i in range(pairs):
                piece = res[:, i * lanes : (i + 1) * lanes].reshape(rows, chunk, lanes)
                qkv_s[n * pairs + i, :, cols, :] = piece
                qkv_ref[n * pairs + i] = piece

    @pl.when(step >= first_steps)
    def _():
        number = step - first_steps
        row = number // pairs
        pair = number % pairs

        @pl.when(pair == 0)
        def _():
            attention_masks(lengths_ref, pad_ref, row, bias_s, qx_s, kx_s, block, False)

        attention_forward(
            qkv_s[pair, row], qkv_s[pairs + pair, row], qkv_s[2 * pairs + pair, row],
            bias_s, qx_s, kx_s, block, back, att_ref, lse_ref,
        )

    @pl.when(step == last)
    def _():
        for at, item in later:
            if at >= count:
                item()
        for plan in plans[2:]:
            plan.landed()
        for plan in plans:
            plan.sent()


def forward(sizes, lengths, pad_len, x, small, matrices, per_ff, block=256, first_steps=4):
    narrow, rows, seq = x.shape
    width = narrow + 1
    pairs = HEADS // 2
    lanes = width // pairs
    nz, ny, nx = sizes
    devices = nz * ny * nx * 2
    ff = per_ff * devices
    back = -(-(MOST - 1) // block)
    chunk = seq // first_steps
    packed = jax.ShapeDtypeStruct((1, 8, 128), BF16)
    shards = [packed] + [m.reshape(-1, 8, m.shape[1]) for m in matrices]
    every = pl.BlockSpec(memory_space=pl.ANY)
    smem = pl.BlockSpec(memory_space=pltpu.SMEM)
    fixed = lambda *shape: pl.BlockSpec(shape, lambda s: (0,) * len(shape))
    early = lambda s: jnp.minimum(s, first_steps - 1)
    number = lambda s: jnp.maximum(s - first_steps, 0)
    head_pair = pl.BlockSpec((None, None, seq, lanes), lambda s: (number(s) % pairs, number(s) // pairs, 0, 0))
    wide = matrices[0].shape[1]
    outs = pl.pallas_call(
        functools.partial(forward_kernel, sizes, narrow, block, back, first_steps, per_ff),
        grid=(first_steps + rows * pairs,),
        in_specs=[smem, smem, pl.BlockSpec((width, rows, seq), lambda s: (0, 0, 0), pipeline_mode=pl.Buffered(1))]
        + [fixed(*small.shape)]
        + [every] * 4,
        out_specs=[every] * 5
        + [
            fixed(8, width),
            fixed(8, ff),
            pl.BlockSpec((rows, chunk, width), lambda s: (0, early(s), 0)),
            pl.BlockSpec((3 * pairs, rows, chunk, lanes), lambda s: (0, 0, early(s), 0)),
            head_pair,
            head_pair,
        ],
        out_shape=[jax.ShapeDtypeStruct((nz, ny, nx, 2) + s.shape, BF16) for s in shards]
        + [
            jax.ShapeDtypeStruct((8, width), F32),
            jax.ShapeDtypeStruct((8, ff), F32),
            jax.ShapeDtypeStruct((rows, seq, width), BF16),
            jax.ShapeDtypeStruct((3 * pairs, rows, seq, lanes), BF16),
            jax.ShapeDtypeStruct((pairs, rows, seq, lanes), BF16),
            jax.ShapeDtypeStruct((pairs, rows, seq, lanes), F32),
        ],
        scratch_shapes=semaphores(5, len(Gather.keys(nz, nx)), 1)
        + [
            pltpu.VMEM(packed.shape, BF16),
            pltpu.VMEM((nz, ny, nx, 2) + packed.shape, BF16),
            pltpu.VMEM((nz, ny, nx, 2) + shards[1].shape, BF16),
            pltpu.VMEM((width, wide), BF16),
            pltpu.VMEM((rows, seq, width), F32),
            pltpu.VMEM((3 * pairs, rows, seq, lanes), BF16),
            pltpu.VMEM((seq // block, block, block), F32),
            pltpu.VMEM((2, seq, lanes), BF16),
            pltpu.VMEM((2, seq, lanes), BF16),
            pltpu.SemaphoreType.DMA,
        ],
        compiler_params=pltpu.CompilerParams(
            collective_id=1, has_side_effects=True, vmem_limit_bytes=vmem_grant
        ),
        name="forward",
    )(lengths, pad_len, x, small, *shards[1:])
    large = [w.reshape(-1, m.shape[1]) for w, m in zip(outs[1:5], matrices)]
    return large, outs[5:]


def norm_back(d_normed, scaled, factor, gain, width):
    grad_gain = jnp.sum(d_normed * scaled, axis=0, keepdims=True)
    e = d_normed * gain
    d_whole = factor * (e - scaled * (row_sum(e * scaled) / width))
    last = row_sum(jnp.where(lane_index(d_whole.shape) == width - 1, d_whole, 0.0))
    return grad_gain, d_whole, last


def token_block(x_ref, narrow):
    _, rows, chunk = x_ref.shape
    return jnp.concatenate([to_rows(x_ref, m, slice(0, chunk), narrow) for m in range(rows)], axis=0)


def put_block(out_ref, value):
    _, rows, chunk = out_ref.shape
    for m in range(rows):
        from_rows(out_ref, m, slice(0, chunk), value[m * chunk : (m + 1) * chunk])


def beside(ref):
    pieces, rows, chunk, lanes = ref.shape
    return jnp.concatenate([ref[i].reshape(rows * chunk, lanes) for i in range(pieces)], axis=1)


def keep_pieces(ref, start, value):
    lanes = ref.shape[3]
    for i in range(value.shape[1] // lanes):
        piece = value[:, i * lanes : (i + 1) * lanes]
        ref[start // lanes + i] = piece.reshape(ref.shape[1:])


def mlp_kernel(
    narrow, slab,
    x_ref, cot_ref, att_ref, w_out_ref, w_up_ref, w_down_ref, vec_ref, bup_ref,
    out_ref, act_ref, dh_ref, n2_ref, d2_ref, df_ref, dmid_ref, datt_ref, sums_ref, gbu_ref,
):
    width, rows, chunk = x_ref.shape
    ff = w_up_ref.shape[1]
    tokens = rows * chunk
    inside = lane_index((tokens, width)) < narrow
    b_out, gain, b_down = vec_ref[3:4, :], vec_ref[4:5, :], vec_ref[5:6, :]

    @pl.when(pl.program_id(0) == 0)
    def _():
        sums_ref[...] = jnp.zeros_like(sums_ref)
        gbu_ref[...] = jnp.zeros_like(gbu_ref)

    def keep(ref, cols, value):
        ref[:, :, cols] = value.reshape(rows, chunk, -1)

    every = slice(0, width)
    branch = dot(beside(att_ref), w_out_ref[...]) + b_out
    up = token_block(cot_ref, narrow)
    d2 = up - row_sum(up) / width
    grad_b_down = jnp.sum(d2, axis=0, keepdims=True)
    d2 = d2.astype(BF16)
    keep(d2_ref, every, d2)
    branch = branch - row_sum(branch) / width
    middle = jnp.where(inside, token_block(x_ref, narrow) + branch, 0.0)
    whole = jnp.where(inside, middle, -row_sum(middle))
    factor = lax.rsqrt(row_sum(whole * whole) / width + epsilon)
    scaled = whole * factor
    n2 = (scaled * gain).astype(BF16)
    keep(n2_ref, every, n2)

    def stage(n):
        cols = slice(n * slab, (n + 1) * slab)
        return dot(n2, w_up_ref[:, cols]), dot(d2, w_down_ref[cols, :], NT)

    count = ff // slab
    ahead = stage(0)
    for n in range(count):
        cols = slice(n * slab, (n + 1) * slab)
        hidden, d_act = ahead
        if n + 1 < count:
            ahead = stage(n + 1)
        hidden = hidden + bup_ref[6:7, cols]
        square = hidden * hidden
        half = 0.5 + 0.5 * jnp.tanh(hidden * (gelu_c0 + gelu_c1 * square))
        active = hidden * half
        slope = half + active * (1.0 - half) * (2.0 * gelu_c0 + (6.0 * gelu_c1) * square)
        keep_pieces(act_ref, n * slab, active.astype(BF16))
        d_hidden = d_act * slope
        gbu_ref[:, cols] += jnp.sum(d_hidden, axis=0, keepdims=True)
        keep_pieces(dh_ref, n * slab, d_hidden.astype(BF16))
    dn2 = dot(beside(dh_ref), w_up_ref[...], NT)
    b2 = dot(beside(act_ref), w_down_ref[...]) + b_down
    grad_gain, d_whole, last = norm_back(dn2, scaled, factor, gain, width)
    d_mid = jnp.where(inside, up + d_whole - last, 0.0)
    dmid_ref[...] = d_mid.reshape(dmid_ref.shape)
    d_first = d_mid - row_sum(d_mid) / width
    sums_ref[3:4, :] += jnp.sum(d_first, axis=0, keepdims=True)
    sums_ref[4:5, :] += grad_gain
    sums_ref[5:6, :] += grad_b_down
    d_first = d_first.astype(BF16)
    keep(df_ref, every, d_first)
    keep_pieces(datt_ref, 0, dot(d_first, w_out_ref[...], NT).astype(BF16))
    put_block(out_ref, middle + b2 - row_sum(b2) / width)


def mlp(x, cot, att, w_out, w_up, w_down, vectors, b_up, chunk=256, slab=1024, tile=512):
    narrow, rows, seq = x.shape
    width = narrow + 1
    ff = w_up.shape[1]
    per_token = lambda n: pl.BlockSpec((rows, chunk, n), lambda i: (0, i, 0))
    pieces = lambda like: pl.BlockSpec(like.shape[:2] + (chunk,) + like.shape[3:], lambda i: (0, 0, i, 0))
    split = jax.ShapeDtypeStruct((ff // tile, rows, seq, tile), BF16)
    feature_first = pl.BlockSpec((width, rows, chunk), lambda i: (0, 0, i))
    fixed = lambda *shape: pl.BlockSpec(shape, lambda i: (0, 0))
    once = lambda *shape: pl.BlockSpec(shape, lambda i: (0, 0), pipeline_mode=pl.Buffered(1))
    tokens = lambda n, dtype: jax.ShapeDtypeStruct((rows, seq, n), dtype)
    return pl.pallas_call(
        functools.partial(mlp_kernel, narrow, slab),
        grid=(seq // chunk,),
        in_specs=[feature_first, feature_first, pieces(att)]
        + [once(width, width), once(width, ff), once(ff, width), once(8, width), once(8, ff)],
        out_specs=[feature_first, pieces(split), pieces(split)]
        + [per_token(width)] * 4
        + [pieces(att)]
        + [fixed(8, width), fixed(1, ff)],
        out_shape=[
            jax.ShapeDtypeStruct(x.shape, BF16),
            split,
            split,
            tokens(width, BF16),
            tokens(width, BF16),
            tokens(width, BF16),
            tokens(width, F32),
            jax.ShapeDtypeStruct(att.shape, BF16),
            jax.ShapeDtypeStruct((8, width), F32),
            jax.ShapeDtypeStruct((1, ff), F32),
        ],
        compiler_params=pltpu.CompilerParams(vmem_limit_bytes=vmem_grant),
        name="mlp",
    )(x, cot, att, w_out, w_up, w_down, vectors, b_up)


def attention_backward(
    docs, q, k, v, att, d_att, lse, bias_ref, qx_ref, kx_ref, dq_s, block, back, dq_ref, dk_ref, dv_ref
):
    seq, lanes = q.shape
    head = lanes // 2
    lane = lane_index((seq, lanes))
    q = q * jnp.asarray(head**-0.5, BF16)
    product = d_att.astype(F32) * att.astype(F32)
    high = product.astype(BF16)
    low = (product - high.astype(F32)).astype(BF16)
    r = lax.broadcasted_iota(jnp.int32, (lanes, lanes), 0)
    c = lax.broadcasted_iota(jnp.int32, (lanes, lanes), 1)
    swap = jnp.where((r < head) != (c < head), 1.0, 0.0).astype(BF16)
    delta = split3(-(dot(high, swap) + dot(low, swap)))
    minus_lse = split3(-pltpu.roll(lse, head, 1))
    own = [lane < head, lane >= head]
    queries, keys, values, upstream = [], [], [], []
    for h in range(2):
        spare = lane - (1 - h) * head
        qx = qx_ref[h]
        dx = jnp.zeros_like(d_att)
        for n in range(3):
            qx = jnp.where(spare == docs + 1 + n, minus_lse[n], qx)
            dx = jnp.where(spare == n, delta[n], dx)
        vx = jnp.where((spare >= 0) & (spare < 3), 1.0, 0.0).astype(BF16)
        queries.append(jnp.where(own[h], q, qx))
        keys.append(jnp.where(own[h], k, kx_ref[h]))
        values.append(jnp.where(own[h], v, vx))
        upstream.append(jnp.where(own[h], d_att, dx))
        dq_s[h] = jnp.zeros((seq, lanes), F32)
    units = []
    for j in range(seq // block):
        for h in range(2):
            units.append((j, h, j * block, (j + 1) * block, min(seq, (j + 1 + back) * block)))

    def products(unit):
        _, h, start, stop, top = unit
        return (
            dot(keys[h][start:stop], queries[h][start:top], NT),
            dot(values[h][start:stop], upstream[h][start:top], NT),
        )

    left = lane[:block] < head
    sum_values = jnp.zeros((1, lanes), F32)
    ahead = products(units[0])
    for n, (j, h, start, stop, top) in enumerate(units):
        scores, d_probs = ahead
        if n + 1 < len(units):
            ahead = products(units[n + 1])
        near = scores[:, :block] + bias_ref[j]
        scores = jnp.concatenate([near, scores[:, block:]], axis=1) if top > stop else near
        probs = jnp.exp(scores)
        d_scores = (probs * d_probs).astype(BF16)
        d_values = dot(probs.astype(BF16), d_att[start:top])
        d_keys = dot(d_scores, q[start:top])
        dq_s[h, start:top, :] += dot(d_scores, k[start:stop], TN)
        if h == 0:
            first = (d_values, d_keys)
        else:
            d_values = jnp.where(left, first[0], d_values)
            sum_values = sum_values + jnp.sum(d_values, axis=0, keepdims=True)
            dv_ref[start:stop, :] = d_values.astype(BF16)
            dk_ref[start:stop, :] = jnp.where(left, first[1], d_keys).astype(BF16)
    d_query = jnp.where(lane < head, dq_s[0], dq_s[1]) * head**-0.5
    dq_ref[...] = d_query.astype(BF16)
    return jnp.sum(d_query, axis=0, keepdims=True), sum_values


class Sums(Scatter):
    @staticmethod
    def buffers(nz, n2, block, dtype):
        return Scatter.buffers(nz, n2, block, dtype)[1:]

    def __init__(self, place, terms, out, buffers, send, recv):
        Transfer.__init__(self, place, send, recv)
        self.terms, self.out = terms, out
        self.r0, self.r1, self.r2, self.r3 = buffers
        self.slabs = out.shape[0]

    def term(self, a, b, d, other_core=False):
        p = self.place
        wide, narrow = p.device(a, b, d, other_core)
        device = wide * (p.nx * 2) + narrow
        return self.terms.at[pl.ds(device * self.slabs, self.slabs)]

    def ends(self, key):
        p = self.place
        kind = key[0]
        if kind == "c":
            a, b, d = key[1:]
            return self.term(a, b, d, True), self.r0.at[self.slot(b, a, d)], p.device(0, 0, 0, True)
        if kind == "t":
            a, b, d = key[1:]
            return self.term(a, b, d), self.r1.at[self.slot(a - 1, b, d)], p.device(a, 0, 0)
        if kind == "s":
            b, d = key[1:]
            return self.term(0, b, d), self.r2.at[self.slot(0, b - 1, d)], p.device(0, b, 0)
        return self.term(0, 0, key[1]), self.r3.at[key[1] - 1], p.device(0, 0, key[1])

    def begin(self):
        for a, b, d in self.order():
            self.start("c", b, a, d)

    def gathered(self, a, b, d):
        p = self.place
        self.arrived("c", b, a, d)
        parts = [self.term(a, b, d), self.r0.at[self.slot(a, b, d)]]
        if a == 0:
            for k in range(1, p.nx):
                self.arrived("t", k, b, d)
                parts.append(self.r1.at[self.slot(k - 1, b, d)])
            if b == 0:
                for k in range(1, p.nx):
                    self.arrived("s", k, d)
                    parts.append(self.r2.at[self.slot(0, k - 1, d)])
        return parts


def as_slabs(value):
    return value.reshape(-1, 8, value.shape[1]).astype(BF16)


def backward_times(tiles, steps, per_chunk):
    a = 2 * tiles + 1
    spread = lambda start, stop, n: [start + (stop - start) * i // n for i in range(n)]
    return [
        (tiles, spread(tiles + 1, 2 * tiles - 2, 8), spread(a + 1, a + 2, 4), spread(a + 3, a + 4, 3), a + 8),
        (2 * tiles, spread(a + 1, a + 2, 8), spread(a + 4, a + 5, 4), spread(a + 6, a + 7, 3), a + 11),
        (a, spread(a + 3, a + 4, 8), spread(a + 6, a + 7, 4), spread(a + 7, a + 8, 3), a + 10),
        (a + per_chunk, spread(a + per_chunk + 1, a + per_chunk + 2, 8), [a + 8] * 4, [a + 9] * 3, a + 11),
        (a + 2 * per_chunk, [a + 2 * per_chunk + 1] * 8, [a + 10] * 4, [a + 11] * 3, steps),
    ]


def stage_steps(plan, times):
    nz, n2 = plan.place.nz, plan.place.nx
    counts = (nz * n2 * (n2 - 1), nz * (n2 - 1), nz - 1, 1)
    items = plan.steps()
    due = []
    for stage, count in zip(times[1:], counts):
        stage = stage if isinstance(stage, list) else [stage]
        due += [stage[m * len(stage) // count] for m in range(count)]
    return list(zip(due, items))


def backward_kernel(
    sizes, block, back, tiles, chunks,
    lengths_ref, pad_ref, act_ref, dh_ref, d2_ref, n2_ref, att_all, df_ref, n1_ref,
    q_ref, k_ref, v_ref, att_ref, datt_ref, lse_ref,
    dq_out, dk_out, dv_out, sq_ref, sv_ref, left_ref, *refs,
):
    kept = chunks - 1
    count = 3 + kept
    outs, refs = refs[:count], refs[count:]
    send, recv, bias_s, qx_s, kx_s, dq_s, pair_s, x_s, y_s, z_s, load = refs[:11]
    terms, bufs = refs[11 : 11 + count], refs[11 + count :]
    step = pl.program_id(0)
    rows, seq, width = x_s.shape
    tokens = rows * seq
    place = Place(*sizes)
    plans = [
        Sums(place, terms[n], outs[n], bufs[4 * n : 4 * n + 4], send.at[n], recv.at[n]) for n in range(count)
    ]
    first = 2 * tiles + 1
    pairs = (3 * width) // (3 * q_ref.shape[1])
    per_chunk = rows * pairs // chunks
    steps = first + rows * pairs
    times = backward_times(tiles, steps, per_chunk)
    due = []
    for n, plan in enumerate(plans):
        due.append((times[n][0], plan.begin))
        due += stage_steps(plan, times[n])
    flat = lambda ref: ref[...].reshape(tokens, -1)
    fetch = lambda source, target, n: pltpu.make_async_copy(source, target, load.at[n])

    @pl.when(step == 0)
    def _():
        place.greet()
        fetch(d2_ref, x_s, 0).start()
        fetch(n2_ref, y_s, 1).start()
        fetch(att_all, z_s, 2).start()
        fetch(d2_ref, x_s, 0).wait()

    @pl.when(step == tiles)
    def _():
        fetch(df_ref, x_s, 0).start()
        fetch(n2_ref, y_s, 1).wait()

    @pl.when(step == 2 * tiles)
    def _():
        fetch(n1_ref, y_s, 1).start()
        fetch(att_all, z_s, 2).wait()
        fetch(df_ref, x_s, 0).wait()

    @pl.when(step == first)
    def _():
        fetch(n1_ref, y_s, 1).wait()

    for n in range(steps):
        some = [item for at, item in due if at == n]
        if some:

            @pl.when(step == n)
            def _():
                for item in some:
                    item()

    @pl.when(step < tiles)
    def _():
        tile = as_slabs(dot(flat(act_ref), flat(x_s), TN))
        terms[0][pl.ds(step * tile.shape[0], tile.shape[0])] = tile

    @pl.when((step >= tiles) & (step < 2 * tiles))
    def _():
        tile = as_slabs(dot(flat(y_s), flat(dh_ref), TN))
        lanes = tile.shape[2]
        terms[1][:, :, pl.ds(pl.multiple_of((step - tiles) * lanes, lanes), lanes)] = tile

    @pl.when(step == 2 * tiles)
    def _():
        terms[2][...] = as_slabs(dot(beside(z_s), flat(x_s), TN))

    @pl.when(step >= first)
    def _():
        number = step - first
        row = number % rows
        lanes = q_ref.shape[1]

        @pl.when(number < rows)
        def _():
            attention_masks(lengths_ref, pad_ref, row, bias_s.at[row], qx_s.at[row], kx_s.at[row], block, True)

        sum_query, sum_values = attention_backward(
            lengths_ref.shape[1], q_ref[...], k_ref[...], v_ref[...], att_ref[...], datt_ref[...], lse_ref[...],
            bias_s.at[row], qx_s.at[row], kx_s.at[row], dq_s, block, back,
            pair_s.at[0, row], pair_s.at[1, row], pair_s.at[2, row],
        )
        for n, ref in enumerate((dq_out, dk_out, dv_out)):
            ref[...] = pair_s[n, row]

        @pl.when(row == 0)
        def _():
            sq_ref[...] = sum_query
            sv_ref[...] = sum_values

        @pl.when(row > 0)
        def _():
            sq_ref[...] += sum_query
            sv_ref[...] += sum_values

    per = pairs // chunks
    for pair in range(pairs):

        @pl.when(step == first + rows * pair + rows - 1)
        def _():
            lanes = q_ref.shape[1]
            right = jnp.concatenate([pair_s[n].reshape(tokens, lanes) for n in range(3)], axis=1)
            tile = as_slabs(dot(flat(y_s), right, TN))
            target = terms[3 + pair // per] if pair // per < kept else left_ref
            target[:, :, (pair % per) * 3 * lanes : (pair % per + 1) * 3 * lanes] = tile

    @pl.when(step == steps - 1)
    def _():
        for at, item in due:
            if at >= steps:
                item()
        for plan in plans:
            plan.sent()


def backward(
    sizes, lengths, pad_len, active, d_hidden, d_second, normed_second, attended, d_first, normed_first, qkv, d_attended,
    log_sums, block=256, chunks=3,
):
    nz, ny, nx = sizes
    pairs, rows, seq, lanes = attended.shape
    width = pairs * lanes
    tiles, tile = active.shape[0], active.shape[3]
    ff = tiles * tile
    devices = nz * ny * nx * 2
    back = -(-(MOST - 1) // block)
    first = 2 * tiles + 1
    steps = first + rows * pairs
    every = pl.BlockSpec(memory_space=pl.ANY)
    smem = pl.BlockSpec(memory_space=pltpu.SMEM)
    number = lambda s: jnp.maximum(s - first, 0)
    head_pair = pl.BlockSpec((None, None, seq, lanes), lambda s: (number(s) // rows, number(s) % rows, 0, 0))
    kind = lambda n: pl.BlockSpec((None, None, seq, lanes), lambda s: (n * pairs + number(s) // rows, number(s) % rows, 0, 0))
    sums = pl.BlockSpec((1, lanes), lambda s: (0, number(s) // rows))
    part = [(ff, width), (width, ff), (width, width)] + [(width, 3 * width // chunks)] * (chunks - 1)
    blocks = [(m // devices // 8, 8, n) for m, n in part]
    left = (width // 8, 8, 3 * width // chunks)
    fixed = lambda shape: pl.BlockSpec(shape, lambda s: (0,) * len(shape), pipeline_mode=pl.Buffered(1))
    bufs = []
    for b in blocks:
        bufs += Sums.buffers(nz, nx, b, BF16)
    keys = len(Scatter.keys(nz, nx))
    token = jax.ShapeDtypeStruct(attended.shape, BF16)
    held = pltpu.VMEM((rows, seq, width), BF16)
    outs = pl.pallas_call(
        functools.partial(backward_kernel, sizes, block, back, tiles, chunks),
        grid=(steps,),
        in_specs=[
            smem,
            smem,
            pl.BlockSpec((None, rows, seq, tile), lambda s: (jnp.minimum(s, tiles - 1), 0, 0, 0)),
            pl.BlockSpec((None, rows, seq, tile), lambda s: (jnp.clip(s - tiles, 0, tiles - 1), 0, 0, 0)),
        ]
        + [every] * 5
        + [kind(0), kind(1), kind(2), head_pair, head_pair, head_pair],
        out_specs=[head_pair, head_pair, head_pair, sums, sums, fixed(left)] + [fixed(b) for b in blocks],
        out_shape=[token, token, token]
        + [jax.ShapeDtypeStruct((1, width), F32)] * 2
        + [jax.ShapeDtypeStruct(left, BF16)]
        + [jax.ShapeDtypeStruct(b, F32) for b in blocks],
        scratch_shapes=semaphores(len(blocks), keys, 1)[:2]
        + [
            pltpu.VMEM((rows, seq // block, block, block), F32),
            pltpu.VMEM((rows, 2, seq, lanes), BF16),
            pltpu.VMEM((rows, 2, seq, lanes), BF16),
            pltpu.VMEM((2, seq, lanes), F32),
            pltpu.VMEM((3, rows, seq, lanes), BF16),
            held,
            held,
            pltpu.VMEM(attended.shape, BF16),
            pltpu.SemaphoreType.DMA((3,)),
        ]
        + [pltpu.VMEM((b[0] * devices,) + b[1:], BF16) for b in blocks]
        + bufs,
        compiler_params=pltpu.CompilerParams(
            collective_id=2, has_side_effects=True, vmem_limit_bytes=62 << 20
        ),
        name="backward",
    )(
        lengths, pad_len, active, d_hidden, d_second, normed_second, attended, d_first, normed_first,
        qkv, qkv, qkv, attended, d_attended, log_sums,
    )
    return outs


def collect_vectors(whole, per, lanes):
    width = whole.shape[1]
    devices = width // per
    column = lax.broadcasted_iota(jnp.int32, (devices, 8, width), 2)
    owner = ((column.astype(F32) + 0.5) * (1.0 / per)).astype(jnp.int32)
    device = lax.broadcasted_iota(jnp.int32, (devices, 8, width), 0)
    masked = jnp.where(owner == device, whole[None], 0.0).reshape(devices * 8, width)
    row = lax.broadcasted_iota(jnp.int32, (width, lanes), 0)
    place = row - ((row.astype(F32) + 0.5) * (1.0 / per)).astype(jnp.int32) * per
    hot = jnp.where(place == lane_index((width, lanes)), 1.0, 0.0).astype(BF16)
    return sum(dot(part, hot) for part in split3(masked)).reshape(devices, 8, lanes)


def back_kernel(
    sizes, narrow, per, per_ff,
    x_ref, dq_ref, dk_ref, dv_ref, w_ref, vec_ref, dmid_ref, sums_ref, sq_ref, sv_ref, gbu_ref, left_ref, *refs,
):
    count = len(refs) - 3 - 9 - 8
    done, refs = refs[:count], refs[count:]
    out_ref, wqkv_out, small_out = refs[:3]
    send, recv, small_send, small_recv, load, terms, total, small_terms, small_total = refs[3:12]
    bufs = refs[12:]
    step = pl.program_id(0)
    width, rows, chunk = x_ref.shape
    tokens = rows * chunk
    place = Place(*sizes)
    plan = Sums(place, terms, total, bufs[:4], send, recv)
    small = Sums(place, small_terms, small_total, bufs[4:], small_send, small_recv)
    fetch = pltpu.make_async_copy(left_ref, terms, load)
    grouped = []
    for one, two in zip(plan.steps(), small.steps()):
        grouped += [one, two]
    n2, nz = place.nx, place.nz
    ends = [0, 2 * nz * n2 * (n2 - 1), 2 * nz * n2 * n2 - 2 * nz, 2 * nz * n2 * n2 - 2, len(grouped)]

    @pl.when(step == 0)
    def _():
        fetch.start()
        place.greet()
        row = lax.broadcasted_iota(jnp.int32, sums_ref.shape, 0)
        whole = sums_ref[...] + jnp.where(row == 1, sq_ref[...], 0.0) + jnp.where(row == 2, sv_ref[...], 0.0)
        fetch.wait()
        plan.begin()
        pieces = collect_vectors(whole, per, small_terms.shape[2])
        row = lax.broadcasted_iota(jnp.int32, (8, gbu_ref.shape[1]), 0)
        pieces = pieces + collect_vectors(jnp.where(row == 6, gbu_ref[...], 0.0), per_ff, small_terms.shape[2])
        small_terms[...] = pieces
        small.begin()

    for n in range(3):

        @pl.when(step == n)
        def _():
            for item in grouped[ends[n] : ends[n + 1]]:
                item()

    dn = sum(
        dot(beside(ref), w_ref[:, n * width : (n + 1) * width], NT)
        for n, ref in enumerate((dq_ref, dk_ref, dv_ref))
    )
    x = token_block(x_ref, narrow)
    inside = lane_index(x.shape) < narrow
    whole = jnp.where(inside, x, -row_sum(x))
    factor = lax.rsqrt(row_sum(whole * whole) / width + epsilon)
    _, d_whole, last = norm_back(dn, whole * factor, factor, vec_ref[0:1, :], width)
    out_ref[...] = (dmid_ref[...].reshape(tokens, width) + d_whole - last).astype(BF16).reshape(out_ref.shape)

    @pl.when(step == pl.num_programs(0) - 1)
    def _():
        for item in grouped[ends[3] :]:
            item()
        chunks = list(done) + [total]
        lanes = 2 * (width // HEADS)
        pairs = chunks[0].shape[2] // (3 * lanes)
        for c, source in enumerate(chunks):
            for p in range(pairs):
                for n in range(3):
                    at = n * width + (c * pairs + p) * lanes
                    start = (p * 3 + n) * lanes
                    wqkv_out[:, :, at : at + lanes] = source[:, :, start : start + lanes]
        small_out[...] = small_total[0]
        plan.sent()
        small.sent()


def back(sizes, x, dq, dk, dv, w_qkv, vectors, dmid, sums, sq, sv, gbu, left, done, chunk=256):
    nz, ny, nx = sizes
    narrow, rows, seq = x.shape
    width = narrow + 1
    devices = nz * ny * nx * 2
    ff = gbu.shape[1]
    per, per_ff = width // devices, ff // devices
    per_token = pl.BlockSpec((rows, chunk, width), lambda i: (0, i, 0))
    feature_first = pl.BlockSpec((width, rows, chunk), lambda i: (0, 0, i))
    fixed = lambda shape: pl.BlockSpec(shape, lambda i: (0,) * len(shape), pipeline_mode=pl.Buffered(1))
    keys = len(Scatter.keys(nz, nx))
    block = (left.shape[0] // devices,) + left.shape[1:]
    slab = (block[0], 8, 3 * width)
    return pl.pallas_call(
        functools.partial(back_kernel, sizes, narrow, per, per_ff),
        grid=(seq // chunk,),
        in_specs=[feature_first]
        + [pl.BlockSpec(dq.shape[:2] + (chunk,) + dq.shape[3:], lambda i: (0, 0, i, 0))] * 3
        + [fixed((width, 3 * width)), fixed((8, width)), per_token]
        + [fixed((8, width)), fixed((1, width)), fixed((1, width)), fixed((1, ff)), pl.BlockSpec(memory_space=pl.ANY)]
        + [fixed(d.shape) for d in done],
        out_specs=[per_token, fixed(slab), fixed((8, 128))],
        out_shape=[
            jax.ShapeDtypeStruct((rows, seq, width), BF16),
            jax.ShapeDtypeStruct(slab, F32),
            jax.ShapeDtypeStruct((8, 128), F32),
        ],
        scratch_shapes=[pltpu.SemaphoreType.DMA((keys,))] * 4
        + [
            pltpu.SemaphoreType.DMA,
            pltpu.VMEM(left.shape, BF16),
            pltpu.VMEM(block, F32),
            pltpu.VMEM((devices, 8, 128), F32),
            pltpu.VMEM((1, 8, 128), F32),
        ]
        + Sums.buffers(nz, nx, block, BF16)
        + Sums.buffers(nz, nx, (1, 8, 128), F32),
        compiler_params=pltpu.CompilerParams(
            collective_id=3, has_side_effects=True, vmem_limit_bytes=vmem_grant
        ),
        name="back",
    )(x, dq, dk, dv, w_qkv, vectors, dmid, sums, sq, sv, gbu, left, *done)


def finish_kernel(small_ref, wqkv_ref, own_ref, gain_ref, x_ref, *refs):
    count = (len(refs) - 8) // 2
    shards, out_ref, wqkv_out, gain_out = refs[:count], refs[count], refs[count + 1], refs[count + 2]
    outs, smalls = refs[count + 3 : 2 * count + 3], refs[2 * count + 3 :]
    rows = x_ref.shape[0]
    for m in range(rows):
        from_rows(out_ref, m, slice(0, x_ref.shape[1]), x_ref[m].astype(F32))

    @pl.when(pl.program_id(0) == 0)
    def _():
        grad = wqkv_ref[...].reshape(wqkv_out.shape)
        wqkv_out[...] = grad
        total = jnp.broadcast_to(row_sum(grad * own_ref[...].astype(F32)), (grad.shape[0], 128)).T
        gain_out[...] = total[0:1, : gain_ref.shape[1]] / gain_ref[...].astype(F32)
        for source, target in zip(shards, outs):
            target[...] = source[...].reshape(target.shape)
        for n, target in enumerate(smalls):
            target[...] = small_ref[n + 1 : n + 2, : target.shape[1]]


def finish(small, grad_qkv, w_qkv, gain, grad_x, shards, lengths, narrow, chunk=512):
    rows, seq, width = grad_x.shape
    fixed = lambda shape: pl.BlockSpec(shape, lambda i: (0,) * len(shape), pipeline_mode=pl.Buffered(1))
    flat = lambda s: (s.shape[0] * 8, s.shape[2])
    shapes = [w_qkv.shape, (1, w_qkv.shape[0])] + [flat(s) for s in shards] + [(1, n) for n in lengths]
    operands = [small, grad_qkv, w_qkv, gain]
    return pl.pallas_call(
        finish_kernel,
        grid=(seq // chunk,),
        in_specs=[fixed(v.shape) for v in operands]
        + [pl.BlockSpec((rows, chunk, width), lambda i: (0, i, 0))]
        + [fixed(s.shape) for s in shards],
        out_specs=[pl.BlockSpec((width, rows, chunk), lambda i: (0, 0, i))] + [fixed(s) for s in shapes],
        out_shape=[jax.ShapeDtypeStruct((narrow, rows, seq), BF16)] + [jax.ShapeDtypeStruct(s, F32) for s in shapes],
        compiler_params=pltpu.CompilerParams(vmem_limit_bytes=vmem_grant),
        name="finish",
    )(*operands, grad_x, *shards)


def body(
    sizes,
    resid, lengths, pad_len, gain_attn, w_qkv, b_query, b_value, w_out, b_out, gain_mlp, w_up, b_up, w_down, b_down,
    cotangent,
):
    narrow = resid.shape[3]
    seq = resid.shape[2]
    docs = lengths.shape[2]
    lengths = lengths.reshape(-1, docs)
    pad_len = pad_len.reshape(1, -1)
    x = jnp.transpose(resid.reshape(-1, seq, narrow), (2, 0, 1))
    cot = jnp.transpose(cotangent.reshape(-1, seq, narrow), (2, 0, 1))
    small = [v.reshape(1, -1) for v in (gain_attn, b_query, b_value, b_out, gain_mlp, b_down, b_up)]
    short = -sum(v.shape[1] for v in small) % 128
    small = jnp.concatenate(small + [jnp.zeros((1, short), BF16)], axis=1)
    large, (vectors, all_b_up, normed_first, qkv, attended, log_sums) = forward(
        sizes, lengths, pad_len, x, small, [w_qkv, w_out, w_up, w_down], b_up.shape[0]
    )
    all_qkv, all_out, all_up, all_down = large
    result, active, d_hidden, normed_second, d_second, d_first, d_middle, d_attended, sums, sum_b_up = mlp(
        x, cot, attended, all_out, all_up, all_down, vectors, all_b_up
    )
    d_query, d_keys, d_values, sum_query, sum_values, left, *shards = backward(
        sizes, lengths, pad_len, active, d_hidden, d_second, normed_second, attended, d_first, normed_first, qkv,
        d_attended, log_sums,
    )
    grad_tokens, grad_qkv, grad_small = back(
        sizes, x, d_query, d_keys, d_values, all_qkv, vectors, d_middle, sums, sum_query, sum_values, sum_b_up, left,
        shards[3:],
    )
    lengths = [v.shape[0] for v in (b_query, b_value, b_out, gain_mlp, b_down, b_up)]
    grad_x, grad_w_qkv, *grads = finish(
        grad_small, grad_qkv, w_qkv, gain_attn.reshape(1, -1), grad_tokens, shards[:3], lengths, narrow
    )
    grad_gain_attn, grad_w_down, grad_w_up, grad_w_out, *grads = grads
    grad_gain_attn, *grads = [g.reshape(-1) for g in [grad_gain_attn] + grads]
    grad_b_query, grad_b_value, grad_b_out, grad_gain_mlp, grad_b_down, grad_b_up = grads
    as_rows = lambda v: jnp.transpose(v, (1, 2, 0)).reshape(resid.shape)
    return (
        as_rows(result),
        as_rows(grad_x),
        grad_gain_attn,
        grad_w_qkv,
        grad_b_query,
        grad_b_value,
        grad_w_out,
        grad_b_out,
        grad_gain_mlp,
        grad_w_up,
        grad_b_up,
        grad_w_down,
        grad_b_down,
    )


def load_padded(ref, lane, narrow):
    return jnp.where(lane < narrow, ref[...].astype(F32), 0.0)


def norm_qkv_kernel(narrow, x_ref, gain_ref, w_ref, bias_ref, normed_ref, qkv_ref):
    rows, width = x_ref.shape
    lane = lane_index((rows, width))
    x = load_padded(x_ref, lane, narrow)
    whole = jnp.where(lane < narrow, x, -row_sum(x))
    factor = lax.rsqrt(row_sum(whole * whole) / width + epsilon)
    normed = (whole * factor * gain_ref[...]).astype(BF16)
    normed_ref[...] = normed
    for n in range(w_ref.shape[1] // width):
        cols = slice(n * width, (n + 1) * width)
        qkv_ref[:, cols] = (dot(normed, w_ref[:, cols]) + bias_ref[:, cols]).astype(BF16)


def norm_qkv(x, gain, w_qkv, bias, block=512):
    tokens, narrow = x.shape
    width = narrow + 1
    wide = w_qkv.shape[1]
    return pl.pallas_call(
        functools.partial(norm_qkv_kernel, narrow),
        grid=(tokens // block,),
        in_specs=[
            pl.BlockSpec((block, width), lambda i: (i, 0)),
            pl.BlockSpec((1, width), lambda i: (0, 0)),
            pl.BlockSpec((width, wide), lambda i: (0, 0)),
            pl.BlockSpec((1, wide), lambda i: (0, 0)),
        ],
        out_specs=[
            pl.BlockSpec((block, width), lambda i: (i, 0)),
            pl.BlockSpec((block, wide), lambda i: (i, 0)),
        ],
        out_shape=[
            jax.ShapeDtypeStruct((tokens, width), BF16),
            jax.ShapeDtypeStruct((tokens, wide), BF16),
        ],
        compiler_params=pltpu.CompilerParams(vmem_limit_bytes=vmem_grant),
        name="norm_qkv",
    )(x, gain, w_qkv, bias)


def plain_mlp_kernel(
    narrow, chunk,
    x_ref, cot_ref, att_ref, w_out_ref, w_up_ref, w_down_ref, b_out_ref, gain_ref, b_up_ref, b_down_ref,
    out_ref, act_ref, dh_ref, n2_ref, d2_ref, df_ref, dmid_ref, datt_ref, gbd_ref, gbu_ref, gg_ref, gbo_ref,
):
    rows, width = x_ref.shape
    ff = w_up_ref.shape[1]
    lane = lane_index((rows, width))
    inside = lane < narrow

    @pl.when(pl.program_id(0) == 0)
    def _():
        for ref in (gbd_ref, gbu_ref, gg_ref, gbo_ref):
            ref[...] = jnp.zeros_like(ref)

    branch = dot(att_ref[...], w_out_ref[...]) + b_out_ref[...]
    up = load_padded(cot_ref, lane, narrow)
    d2 = up - row_sum(up) / width
    gbd_ref[...] += jnp.sum(d2, axis=0, keepdims=True)
    d2 = d2.astype(BF16)
    d2_ref[...] = d2
    branch = branch - row_sum(branch) / width
    middle = jnp.where(inside, load_padded(x_ref, lane, narrow) + branch, 0.0)
    whole = jnp.where(inside, middle, -row_sum(middle))
    factor = lax.rsqrt(row_sum(whole * whole) / width + epsilon)
    scaled = whole * factor
    n2 = (scaled * gain_ref[...]).astype(BF16)
    n2_ref[...] = n2

    def stage(n):
        cols = slice(n * chunk, (n + 1) * chunk)
        return dot(n2, w_up_ref[:, cols]), dot(d2, w_down_ref[cols, :], NT)

    count = ff // chunk
    ahead = stage(0)
    for n in range(count):
        cols = slice(n * chunk, (n + 1) * chunk)
        hidden, d_act = ahead
        if n + 1 < count:
            ahead = stage(n + 1)
        hidden = hidden + b_up_ref[:, cols]
        square = hidden * hidden
        half = 0.5 + 0.5 * jnp.tanh(hidden * (gelu_c0 + gelu_c1 * square))
        active = hidden * half
        slope = half + active * (1.0 - half) * (2.0 * gelu_c0 + (6.0 * gelu_c1) * square)
        act_ref[:, cols] = active.astype(BF16)
        d_hidden = d_act * slope
        gbu_ref[:, cols] += jnp.sum(d_hidden, axis=0, keepdims=True)
        dh_ref[:, cols] = d_hidden.astype(BF16)
    dn2 = dot(dh_ref[...], w_up_ref[...], NT)
    b2 = dot(act_ref[...], w_down_ref[...]) + b_down_ref[...]
    gg_ref[...] += jnp.sum(dn2 * scaled, axis=0, keepdims=True)
    e = dn2 * gain_ref[...]
    dwhole = factor * (e - scaled * (row_sum(e * scaled) / width))
    last = row_sum(jnp.where(lane == narrow, dwhole, 0.0))
    d_mid = jnp.where(inside, up + dwhole - last, 0.0)
    dmid_ref[...] = d_mid
    d_first = d_mid - row_sum(d_mid) / width
    gbo_ref[...] += jnp.sum(d_first, axis=0, keepdims=True)
    d_first = d_first.astype(BF16)
    df_ref[...] = d_first
    datt_ref[...] = dot(d_first, w_out_ref[...], NT).astype(BF16)
    out_ref[...] = (middle + b2 - row_sum(b2) / width).astype(BF16)


def plain_mlp(x, cot, att, w_out, w_up, w_down, b_out, gain, b_up, b_down, block=256, chunk=512):
    tokens, narrow = x.shape
    width = narrow + 1
    ff = w_up.shape[1]
    per_token = lambda n: pl.BlockSpec((block, n), lambda i: (i, 0))
    fixed = lambda *shape: pl.BlockSpec(shape, lambda i: (0, 0))
    return pl.pallas_call(
        functools.partial(plain_mlp_kernel, narrow, chunk),
        grid=(tokens // block,),
        in_specs=[per_token(width)] * 3
        + [fixed(width, width), fixed(width, ff), fixed(ff, width)]
        + [fixed(1, width), fixed(1, width), fixed(1, ff), fixed(1, width)],
        out_specs=[per_token(width), per_token(ff), per_token(ff)]
        + [per_token(width)] * 5
        + [fixed(1, width), fixed(1, ff), fixed(1, width), fixed(1, width)],
        out_shape=[
            jax.ShapeDtypeStruct((tokens, narrow), BF16),
            jax.ShapeDtypeStruct((tokens, ff), BF16),
            jax.ShapeDtypeStruct((tokens, ff), BF16),
            jax.ShapeDtypeStruct((tokens, width), BF16),
            jax.ShapeDtypeStruct((tokens, width), BF16),
            jax.ShapeDtypeStruct((tokens, width), BF16),
            jax.ShapeDtypeStruct((tokens, width), F32),
            jax.ShapeDtypeStruct((tokens, width), BF16),
            jax.ShapeDtypeStruct((1, width), F32),
            jax.ShapeDtypeStruct((1, ff), F32),
            jax.ShapeDtypeStruct((1, width), F32),
            jax.ShapeDtypeStruct((1, width), F32),
        ],
        compiler_params=pltpu.CompilerParams(vmem_limit_bytes=vmem_grant),
        name="mlp",
    )(x, cot, att, w_out, w_up, w_down, b_out, gain, b_up, b_down)


def wgrad_kernel(left_ref, right_ref, out_ref):
    out_ref[...] = dot(left_ref[...], right_ref[...], TN).astype(out_ref.dtype)


def wgrad(left, right, rows, cols):
    tokens, m = left.shape
    n = right.shape[1]
    return pl.pallas_call(
        wgrad_kernel,
        grid=(m // rows, n // cols),
        in_specs=[
            pl.BlockSpec((tokens, rows), lambda i, j: (0, i)),
            pl.BlockSpec((tokens, cols), lambda i, j: (0, j)),
        ],
        out_specs=pl.BlockSpec((rows, cols), lambda i, j: (i, j)),
        out_shape=jax.ShapeDtypeStruct((m, n), BF16),
        compiler_params=pltpu.CompilerParams(vmem_limit_bytes=vmem_grant),
        name="wgrad",
    )(left, right)


def plain_back_kernel(
    narrow, x_ref, dq_ref, dk_ref, dv_ref, w_ref, gain_ref, dmid_ref, out_ref, gg_ref
):
    rows, width = x_ref.shape
    lane = lane_index((rows, width))
    inside = lane < narrow

    @pl.when(pl.program_id(0) == 0)
    def _():
        gg_ref[...] = jnp.zeros_like(gg_ref)

    dn = dot(dq_ref[...], w_ref[:, 0:width], NT)
    dn = dn + dot(dk_ref[...], w_ref[:, width : 2 * width], NT)
    dn = dn + dot(dv_ref[...], w_ref[:, 2 * width : 3 * width], NT)
    x = load_padded(x_ref, lane, narrow)
    whole = jnp.where(inside, x, -row_sum(x))
    factor = lax.rsqrt(row_sum(whole * whole) / width + epsilon)
    scaled = whole * factor
    gg_ref[...] += jnp.sum(dn * scaled, axis=0, keepdims=True)
    e = dn * gain_ref[...]
    dwhole = factor * (e - scaled * (row_sum(e * scaled) / width))
    last = row_sum(jnp.where(lane == narrow, dwhole, 0.0))
    out_ref[...] = (dmid_ref[...] + dwhole - last).astype(BF16)


def plain_back(x, dq, dk, dv, w_qkv, gain, dmid, block=512):
    tokens, narrow = x.shape
    width = narrow + 1
    per_token = lambda n: pl.BlockSpec((block, n), lambda i: (i, 0))
    fixed = lambda *shape: pl.BlockSpec(shape, lambda i: (0, 0))
    return pl.pallas_call(
        functools.partial(plain_back_kernel, narrow),
        grid=(tokens // block,),
        in_specs=[per_token(width)] * 4
        + [fixed(width, 3 * width), fixed(1, width), per_token(width)],
        out_specs=[per_token(width), fixed(1, width)],
        out_shape=[
            jax.ShapeDtypeStruct((tokens, narrow), BF16),
            jax.ShapeDtypeStruct((1, width), F32),
        ],
        compiler_params=pltpu.CompilerParams(vmem_limit_bytes=vmem_grant),
        name="back",
    )(x, dq, dk, dv, w_qkv, gain, dmid)


def fwd_kernel(docs, hd, blk, back, q_ref,k_ref,v_ref,segc_ref,segr_ref,o_ref,lse_ref,bias_ref,qx_ref,kx_ref):
    seq=q_ref.shape[0]; lanes=2*hd
    nb=seq//blk
    pair=pl.program_id(1)
    lane=lax.broadcasted_iota(jnp.int32,(seq,lanes),1)
    @pl.when(pair==0)
    def _():
        segc=segc_ref[...]
        for i in range(nb):
            sq=segc[i*blk:(i+1)*blk]; sk=segr_ref[:,i*blk:(i+1)*blk]
            r=lax.broadcasted_iota(jnp.int32,(blk,blk),0); c=lax.broadcasted_iota(jnp.int32,(blk,blk),1)
            bias_ref[i]=jnp.where((c<=r)&(sq==sk),0.0,masked_score)
        for h in range(2):
            sub=lane-(1-h)*hd
            seg=jnp.broadcast_to(jnp.minimum(segc,docs),(seq,lanes))
            in_aug=(sub>=0)&(sub<=docs)
            hot=seg==sub
            qx_ref[h]=jnp.where(in_aug&~hot,masked_score,0.0).astype(BF16)
            kx_ref[h]=jnp.where(in_aug&hot,1.0,0.0).astype(BF16)
    scale=hd**-0.5
    q=q_ref[...]*jnp.asarray(scale,BF16); k=k_ref[...]; v=v_ref[...]
    own=[lane<hd, lane>=hd]
    qa=[jnp.where(own[h],q,qx_ref[h]) for h in range(2)]
    ka=[jnp.where(own[h],k,kx_ref[h]) for h in range(2)]
    va=[jnp.where(own[h],v,jnp.asarray(1.0,BF16)) for h in range(2)]
    units=[(i,h) for i in range(nb) for h in range(2)]
    kt=[a.T for a in ka]
    def score(u):
        i,h=u
        lo=max(0,i-back)*blk; hi=(i+1)*blk; d0=i*blk
        qb=qa[h][d0:hi]
        parts=[]
        if lo<d0: parts.append(dot(qb,kt[h][:,lo:d0]))
        parts.append(dot(qb,kt[h][:,d0:hi])+bias_ref[i])
        return parts
    nxt=score(units[0])
    keep={}
    for n,(i,h) in enumerate(units):
        lo=max(0,i-back)*blk; hi=(i+1)*blk; d0=i*blk
        parts=nxt
        if n+1<len(units): nxt=score(units[n+1])
        m=functools.reduce(jnp.maximum,[jnp.max(p,axis=1,keepdims=True) for p in parts])
        ps=[jnp.exp(p-m).astype(BF16) for p in parts]
        o=dot(ps[-1],va[h][d0:hi])
        if lo<d0: o=o+dot(ps[0],va[h][lo:d0])
        l=pltpu.roll(o,hd,1)
        keep[h]=(o/l,m+jnp.log(l))
        if h==1:
            ln=lane[:blk]
            o_ref[d0:hi,:]=jnp.where(ln<hd,keep[0][0],keep[1][0]).astype(BF16)
            lse_ref[d0:hi,:]=jnp.where(ln<hd,keep[0][1],keep[1][1])


def attn_fwd(qkv,segments,docs,heads,blk=256,most=512):
    rows,seq=segments.shape; T,w=qkv.shape
    d=w//3; hd=d//heads; lanes=2*hd; pairs=heads//2
    back=-(-(most-1)//blk)
    spec=lambda off: pl.BlockSpec((seq,lanes),lambda r,p:(r,off+p))
    return pl.pallas_call(
        functools.partial(fwd_kernel,docs,hd,blk,back),
        grid=(rows,pairs),
        in_specs=[spec(0),spec(pairs),spec(2*pairs),
                  pl.BlockSpec((None,seq,1),lambda r,p:(r,0,0)),pl.BlockSpec((None,1,seq),lambda r,p:(r,0,0))],
        out_specs=[spec(0),spec(0)],
        out_shape=[jax.ShapeDtypeStruct((T,d),BF16),jax.ShapeDtypeStruct((T,d),F32)],
        scratch_shapes=[pltpu.VMEM((seq//blk,blk,blk),F32),pltpu.VMEM((2,seq,lanes),BF16),pltpu.VMEM((2,seq,lanes),BF16)],
        compiler_params=pltpu.CompilerParams(vmem_limit_bytes=vmem_grant),
    )(qkv,qkv,qkv,segments[:,:,None],segments[:,None,:])

def bwd_kernel(docs, hd, blk, back, q_ref,k_ref,v_ref,o_ref,do_ref,lse_ref,segc_ref,segr_ref,
               dq_ref,dk_ref,dv_ref,sq_ref,sv_ref,bias_ref,qx_ref,kx_ref,dqa_ref):
    seq=q_ref.shape[0]; lanes=2*hd
    nb=seq//blk
    pair=pl.program_id(1)
    lane=lax.broadcasted_iota(jnp.int32,(seq,lanes),1)
    @pl.when(pair==0)
    def _():
        segc=segc_ref[...]
        for i in range(nb):
            sk=segc[i*blk:(i+1)*blk]; sq=segr_ref[:,i*blk:(i+1)*blk]
            r=lax.broadcasted_iota(jnp.int32,(blk,blk),0); c=lax.broadcasted_iota(jnp.int32,(blk,blk),1)
            bias_ref[i]=jnp.where((r<=c)&(sq==sk),0.0,masked_score)
        for h in range(2):
            sub=lane-(1-h)*hd
            seg=jnp.broadcast_to(jnp.minimum(segc,docs),(seq,lanes))
            in_aug=(sub>=0)&(sub<=docs)
            hot=seg==sub
            qx_ref[h]=jnp.where(in_aug&~hot,masked_score,0.0).astype(BF16)
            kx_ref[h]=jnp.where((in_aug&hot)|((sub>docs)&(sub<=docs+3)),1.0,0.0).astype(BF16)
    scale=hd**-0.5
    q=q_ref[...]*jnp.asarray(scale,BF16); k=k_ref[...]; v=v_ref[...]; do=do_ref[...]
    prod=do.astype(F32)*o_ref[...].astype(F32)
    hi_=prod.astype(BF16); lo_=(prod-hi_.astype(F32)).astype(BF16)
    r=lax.broadcasted_iota(jnp.int32,(lanes,lanes),0); c=lax.broadcasted_iota(jnp.int32,(lanes,lanes),1)
    ones=jnp.where((r<hd)!=(c<hd),1.0,0.0).astype(BF16)
    delta=-(dot(hi_,ones)+dot(lo_,ones))
    nl=-pltpu.roll(lse_ref[...],hd,1)
    d3=split3(delta); l3=split3(nl)
    own=[lane<hd, lane>=hd]
    qa=[];ka=[];va=[];da=[]
    one=jnp.asarray(1.0,BF16); zero=jnp.asarray(0.0,BF16)
    for h in range(2):
        sub=lane-(1-h)*hd
        qx=qx_ref[h]
        vx=jnp.where((sub>=0)&(sub<3),1.0,0.0).astype(BF16)
        dx=jnp.zeros_like(do)
        for n in range(3):
            qx=jnp.where(sub==docs+1+n,l3[n],qx)
            dx=jnp.where(sub==n,d3[n],dx)
        qa.append(jnp.where(own[h],q,qx))
        ka.append(jnp.where(own[h],k,kx_ref[h]))
        va.append(jnp.where(own[h],v,vx))
        da.append(jnp.where(own[h],do,dx))
    for h in range(2):
        dqa_ref[h]=jnp.zeros((seq,lanes),F32)
    ln=lane[:blk]
    sv=jnp.zeros((1,lanes),F32)
    units=[]
    for j in range(nb):
        d0=j*blk; hi=(j+1)*blk; top=min(nb,j+1+back)*blk
        for h in range(2):
            units.append((j,h,d0,hi,top))
    def stage(u):
        j,h,d0,hi,top=u
        st=dot(ka[h][d0:hi],qa[h][d0:top],NT)
        dpt=dot(va[h][d0:hi],da[h][d0:top],NT)
        return st,dpt
    look=1
    queue=[stage(u) for u in units[:look]]
    for n,(j,h,d0,hi,top) in enumerate(units):
        st,dpt=queue.pop(0)
        if n+look<len(units): queue.append(stage(units[n+look]))
        st0=st[:,:blk]+bias_ref[j]
        st=jnp.concatenate([st0,st[:,blk:]],axis=1) if top>hi else st0
        pt=jnp.exp(st)
        dst=(pt*dpt).astype(BF16)
        pt=pt.astype(BF16)
        dv=dot(pt,do[d0:top]); dk=dot(dst,q[d0:top])
        dqa_ref[h,d0:top,:]+=dot(dst,k[d0:hi],TN)
        if h==0:
            first=(dv,dk)
        else:
            dvf=jnp.where(ln<hd,first[0],dv)
            sv=sv+jnp.sum(dvf,axis=0,keepdims=True)
            dv_ref[d0:hi,:]=dvf.astype(BF16)
            dk_ref[d0:hi,:]=jnp.where(ln<hd,first[1],dk).astype(BF16)
    dq=jnp.where(lane<hd,dqa_ref[0],dqa_ref[1])*scale
    dq_ref[...]=dq.astype(BF16)
    sq_ref[...]=jnp.sum(dq,axis=0,keepdims=True)
    sv_ref[...]=sv

def attn_bwd(qkv,att,datt,lse,segments,docs,heads,blk=256,most=512):
    rows,seq=segments.shape; T,w=qkv.shape
    d=w//3; hd=d//heads; lanes=2*hd; pairs=heads//2
    back=-(-(most-1)//blk)
    spec=lambda off: pl.BlockSpec((seq,lanes),lambda r,p:(r,off+p))
    vec=pl.BlockSpec((None,1,lanes),lambda r,p:(r,0,p))
    return pl.pallas_call(
        functools.partial(bwd_kernel,docs,hd,blk,back),
        grid=(rows,pairs),
        in_specs=[spec(0),spec(pairs),spec(2*pairs),spec(0),spec(0),spec(0),
                  pl.BlockSpec((None,seq,1),lambda r,p:(r,0,0)),pl.BlockSpec((None,1,seq),lambda r,p:(r,0,0))],
        out_specs=[spec(0),spec(0),spec(0),vec,vec],
        out_shape=[jax.ShapeDtypeStruct((T,d),BF16)]*3+[jax.ShapeDtypeStruct((rows,1,d),F32)]*2,
        scratch_shapes=[pltpu.VMEM((seq//blk,blk,blk),F32),pltpu.VMEM((2,seq,lanes),BF16),pltpu.VMEM((2,seq,lanes),BF16),pltpu.VMEM((2,seq,lanes),F32)],
        compiler_params=pltpu.CompilerParams(vmem_limit_bytes=vmem_grant),
    )(qkv,qkv,qkv,att,datt,lse,segments[:,:,None],segments[:,None,:])


def segment_ids(doc_lengths, pad_count, seq_len):
    docs = doc_lengths.shape[-1]
    upto = jnp.arange(docs)[None, :] <= jnp.arange(docs)[:, None]
    doc_ends = jnp.sum(jnp.where(upto[None], doc_lengths[:, None, :], 0), axis=-1)
    positions = jnp.arange(seq_len, dtype=jnp.int32)
    counted = jnp.sum((doc_ends[:, :, None] <= positions[None, None, :]).astype(jnp.int32), axis=1)
    padding = positions[None, :] >= seq_len - pad_count[:, None]
    return jnp.where(padding, docs + positions[None, :], counted)


def as_row(vector):
    return vector.astype(F32)[None]


def plain_body(
    resid, lengths, pad_len, gain_attn, w_qkv, b_query, b_value, w_out, b_out, gain_mlp, w_up, b_up, w_down, b_down,
    cotangent,
):
    narrow = resid.shape[3]
    width = narrow + 1
    seq = resid.shape[2]
    docs = lengths.shape[2]
    segments = segment_ids(lengths.reshape(-1, docs), pad_len.reshape(-1), seq)
    x = resid.reshape(-1, narrow)
    cot = cotangent.reshape(-1, narrow)
    every = lambda v: lax.all_gather(v, AX, axis=0, tiled=True)
    vectors = [every(v) for v in (gain_attn, b_query, b_value, b_out, gain_mlp, b_down, b_up)]
    matrices = [every(v) for v in (w_qkv, w_out, w_up, w_down)]
    gain_attn, b_query, b_value, b_out, gain_mlp, b_down, b_up = [as_row(v) for v in vectors]
    w_qkv, w_out, w_up, w_down = matrices
    qkv_bias = jnp.concatenate([b_query, jnp.zeros_like(b_query), b_value], axis=1)
    normed_first, qkv = norm_qkv(x, gain_attn, w_qkv, qkv_bias)
    attended, log_sums = attn_fwd(qkv, segments, docs, HEADS, most=MOST)
    (
        result, active, d_hidden, normed_second, d_second, d_first, d_middle, d_attended,
        grad_b_down, grad_b_up, grad_gain_mlp, grad_b_out,
    ) = plain_mlp(x, cot, attended, w_out, w_up, w_down, b_out, gain_mlp, b_up, b_down)
    ff = w_up.shape[1]
    grad_w_down = wgrad(active, d_second, 512, width)
    grad_w_up = wgrad(normed_second, d_hidden, width, 512)
    grad_w_out = wgrad(attended, d_first, width, width)
    d_query, d_keys, d_values, sum_query, sum_value = attn_bwd(
        qkv, attended, d_attended, log_sums, segments, docs, HEADS, most=MOST
    )
    grads_qkv = [wgrad(normed_first, d, width, width) for d in (d_query, d_keys, d_values)]
    grad_input, grad_gain_attn = plain_back(x, d_query, d_keys, d_values, w_qkv, gain_attn, d_middle)
    vectors = [
        grad_gain_attn[0],
        jnp.sum(sum_query, axis=(0, 1)),
        jnp.sum(sum_value, axis=(0, 1)),
        grad_b_out[0],
        grad_gain_mlp[0],
        grad_b_down[0],
        grad_b_up[0],
    ]
    own = lambda v: lax.psum_scatter(v.astype(F32), AX, scatter_dimension=0, tiled=True)
    vectors = [own(v) for v in vectors]
    matrices = [own(v) for v in [grad_w_down, grad_w_up, grad_w_out] + grads_qkv]
    grad_gain_attn, grad_b_query, grad_b_value, grad_b_out, grad_gain_mlp, grad_b_down, grad_b_up = vectors
    grad_w_down, grad_w_up, grad_w_out = matrices[:3]
    grad_w_qkv = jnp.concatenate(matrices[3:], axis=1)
    return (
        result.reshape(resid.shape),
        grad_input.reshape(resid.shape),
        grad_gain_attn,
        grad_w_qkv,
        grad_b_query,
        grad_b_value,
        grad_w_out,
        grad_b_out,
        grad_gain_mlp,
        grad_w_up,
        grad_b_up,
        grad_w_down,
        grad_b_down,
    )


def slice_sizes(mesh, rows):
    wide, narrow = mesh.shape["wide"], mesh.shape["narrow"]
    depth = len({getattr(d, "coords", (0, 0, 0))[1] for d in mesh.devices.flat})
    per = rows // (wide * narrow)
    if per % 8 or 4 * per > 128 or rows % (wide * narrow) or narrow % 2 or depth != narrow // 2 or wide % depth:
        return None
    return (wide // depth, depth, narrow // 2)


def solution(mesh):
    row_split = P(None, AX)
    own = P(AX)

    def program(*args):
        sizes = slice_sizes(mesh, args[3].shape[0])
        return jax.shard_map(
            plain_body if sizes is None else functools.partial(body, sizes),
            mesh=mesh,
            in_specs=(row_split,) * 3 + (own,) * 11 + (row_split,),
            out_specs=(row_split,) * 2 + (own,) * 11,
            check_vma=False,
        )(*args)

    return program
```
